32 devices in a mesh: shard: 8 (over z, x), rep: 4 (over y, core).
Axes of the slice: x: 2, y: 2, z: 4, core: 2. Of those that a mesh axis runs over, the one named last changes fastest.
Arguments:
- grad_pooled: bfloat16 [4096, 8, 128], P(('shard', 'rep')), may hold values from -6 to 6
- lookup_weight: float32 [65536], P(('shard', 'rep')), may hold values from 0.25 to 4
- owner: int32 [65536, 1], P(('shard', 'rep')), may hold values from 0 to 7; in each aligned block of 2048 rows (0 to 2047, 2048 to 4095, ...) at most 384 rows name the same one
- local_row: int32 [65536], P(('shard', 'rep')), may hold values from 0 to 4095
- weight: float32 [32768, 128], P('shard'), may hold values from -6 to 6
- accum: float32 [32768], P('shard'), may hold values from 0.1 to 10
Outputs:
- new_weight: float32 [32768, 128], P('shard')
- new_accum: float32 [32768], P('shard')
The draws below stay inside these ranges and needn't reach their ends.
Inputs may be any that keep to these rules, and one draw needn't show every extreme that they name: Among the lookups of one device no owner is named more than 384 times, a bound that some block reaches.
All inputs are finite; a program needn't handle non-finite values.
Results may differ from the reference program's by a relative error of at most 0.0011.
Values may be sent and summed in bfloat16 or wider, within the bound.
No kernel may reach another device: no remote copies, remote signals or barrier semaphores. Data moves between devices by JAX's collectives and lax.ppermute only.
A program may use at most 64 MiB of HBM per device.

```python
import math
import jax
import jax.numpy as jnp
import numpy as np
from jax import lax

D = 128
SAMPLES = 128
FEAT = 8
POOL = 2
WROWS = 4096
LOOK_DEV = 2048
CAP = 384
BATCH = 4096
LOOKUPS = 65536
ROWS = 32768
N_SHARD = 8


def place_ends(entries, rng, low, high):
    place = [jax.random.randint(jax.random.fold_in(rng, axis), (), 0, length) for axis, length in enumerate(entries.shape)]
    widest = entries.shape.index(max(entries.shape))
    neighbour = place[:widest] + [(place[widest] + 1) % entries.shape[widest]] + place[widest + 1:]
    return entries.at[tuple(place)].set(low).at[tuple(neighbour)].set(high)


def level_of(own_key, shape, split, low, top_value):
    def one(axis_at, parts):
        heights = jax.random.uniform(jax.random.fold_in(jax.random.fold_in(own_key, 6), axis_at), (parts,), jnp.float32, low / len(split), top_value / len(split))
        return jnp.repeat(jnp.exp(heights), shape[axis_at] // parts).reshape((-1,) + (1,) * (len(shape) - axis_at - 1))

    gain = one(*split[0])
    for cut in split[1:]:
        gain = gain * one(*cut)
    return gain


def assign_block(stream_key, own, number, rows, count, top, limit, skew):
    ranking = jax.random.permutation(stream_key, count)
    heavy_load, ordinary = load_shares(count, rows * top, limit, skew, True), load_shares(count, rows * top, limit, skew, False)
    places = jnp.arange(count)

    def named(tallies, rotation):
        used = int((tallies > 0).sum())
        fixed = max(1, used // 4)
        moved = fixed + (places - fixed + rotation * (used - fixed)) % max(1, count - fixed)
        return jnp.zeros((count,), jnp.int32).at[ranking[jnp.where(places < fixed, places, moved)]].set(jnp.asarray(tallies, jnp.int32))

    tallies = jnp.where(number % 4 == 0, named(heavy_load, number // 4), named(ordinary, number - number // 4 - 1))
    mixed = jax.random.permutation(jax.random.fold_in(own, 3), count)
    giver, receiver = mixed[0:count // 2 * 2:2], mixed[1:count // 2 * 2:2]
    room = jnp.minimum(tallies[giver] - 1, limit - tallies[receiver]) // 2
    room = jnp.where((giver == ranking[0]) | (receiver == ranking[0]) | (tallies[receiver] == 0), 0, jnp.maximum(room, 0))
    moved = jax.random.randint(jax.random.fold_in(own, 4), (count // 2,), 0, 1 << 20) % (room + 1)
    tallies = tallies.at[giver].add(-moved).at[receiver].add(moved)
    labels = jnp.searchsorted(jnp.cumsum(tallies), jnp.arange(rows * top), side="right").astype(jnp.int32)
    listing = labels.reshape(top, rows).T
    listing = listing[jax.random.permutation(jax.random.fold_in(own, 1), rows)]
    rotation = jax.random.randint(jax.random.fold_in(own, 2), (rows, 1), 0, top)
    return jnp.take_along_axis(listing, (jnp.arange(top)[None, :] + rotation) % top, axis=1)


def load_shares(amount, total, limit, slope, full):
    loads = [(1 << 20) // math.isqrt(grade ** slope) + 1 for grade in range(1, amount + 1)]
    largest = limit if full else min(limit, max(-(-total // amount), total * loads[0] // sum(loads)))
    least = 1 if total - largest >= amount - 1 else 0
    counts, surplus = [largest] + [least] * (amount - 1), total - largest - least * (amount - 1)
    while surplus > 0:
        free = [i for i in range(1, amount) if counts[i] < largest] or [i for i in range(1, amount) if counts[i] < limit]
        pool, budget = sum([loads[i] for i in free]), surplus
        for i in free:
            extra = min(limit - counts[i], max(1, budget * loads[i] // pool), surplus)
            counts[i] = counts[i] + extra
            surplus = surplus - extra
    return np.array(counts)


def gaussian(own_key, extent, spread, reach, shards=(), dtype=jnp.bfloat16):
    drawn = spread * jax.random.normal(own_key, extent, jnp.float32)
    if shards:
        drawn = drawn * level_of(own_key, extent, shards, -0.22, 0.18)
    return jnp.clip(drawn, -reach, reach).astype(dtype)


def setup_inputs(seed: int = 0) -> dict:
    splits = jax.random.split(jax.random.key(seed), 7)
    grad_pooled = gaussian(splits[0], (BATCH, FEAT, D), 1.0, 6.0, ((0, 32),))
    lookup_weight = jnp.clip(jnp.exp(math.log(4.0) - 2.7725887 * jax.random.uniform(splits[1], (LOOKUPS,), jnp.float32) ** level_of(splits[1], (LOOKUPS,), ((0, 32),), -0.2, 0.2)), 0.25, 4.0)
    owner_keys = jax.random.split(jax.random.fold_in(splits[2], 1), LOOKUPS // LOOK_DEV)
    owner_turns = jax.random.permutation(jax.random.fold_in(splits[2], 3), LOOKUPS // LOOK_DEV)
    owner = jax.vmap(lambda own, number: assign_block(jax.random.fold_in(splits[2], 2), own, number, LOOK_DEV, N_SHARD, 1, CAP, 2))(owner_keys, owner_turns).reshape((LOOKUPS, 1))
    local_row = place_ends(jax.random.randint(splits[3], (LOOKUPS,), 0, WROWS), jax.random.fold_in(splits[3], 1), 0, WROWS - 1).astype(jnp.int32)
    weight = gaussian(splits[4], (ROWS, D), 1.0, 6.0, ((0, 8),), jnp.float32)
    accum = jnp.clip(jnp.exp(math.log(10.0) - 4.6051702 * jax.random.uniform(splits[5], (ROWS,), jnp.float32) ** level_of(splits[5], (ROWS,), ((0, 8),), -0.2, 0.2)), 0.1, 10.0)
    return dict(grad_pooled=grad_pooled, lookup_weight=lookup_weight, owner=owner, local_row=local_row, weight=weight, accum=accum)


step_size = 0.25
epsilon = 1e-08

def reference(grad_pooled, lookup_weight, owner, local_row, weight, accum):
    width = grad_pooled.shape[-1]
    bags = grad_pooled.reshape(-1, SAMPLES * FEAT, width)
    weights = lookup_weight.reshape(-1, SAMPLES * FEAT, POOL)
    target = (owner[:, 0].astype(jnp.int32) * WROWS + local_row.astype(jnp.int32)).reshape(-1, LOOK_DEV)

    def add_device(total, items):
        bag_block, weight_block, target_block = items
        rows = (bag_block.astype(jnp.float32)[:, None, :] * weight_block[:, :, None]).reshape(-1, width)
        rows = rows.astype(jnp.bfloat16)
        return (total.at[target_block].add(rows.astype(jnp.float32)), None)
    start = jnp.zeros((N_SHARD * WROWS, width), jnp.float32)
    table_grad, unused = lax.scan(add_device, start, (bags, weights, target))
    new_accum = accum + lax.optimization_barrier(jnp.mean(table_grad * table_grad, axis=1))
    new_weight = weight - step_size * table_grad / (jnp.sqrt(new_accum)[:, None] + epsilon)
    return (new_weight, new_accum)
```

```python
import functools

import jax
import jax.numpy as jnp
from jax import lax
from jax.experimental import pallas as pl
from jax.experimental.pallas import tpu as pltpu
from jax.sharding import PartitionSpec as P

step_size = 0.25
epsilon = 1e-08
f32, bf16, i32 = jnp.float32, jnp.bfloat16, jnp.int32
LANES = 128
PAD = 16
VMEM_LIMIT = 48 * 1024 * 1024


def adagrad(weight, accum, table_grad):
    new_accum = accum + jnp.mean(table_grad * table_grad, axis=1)
    new_weight = weight - step_size * table_grad / (jnp.sqrt(new_accum)[:, None] + epsilon)
    return (new_weight, new_accum)


def general_body(grad_pooled, lookup_weight, owner, local_row, weight, accum):
    width = grad_pooled.shape[-1]
    lookups = lookup_weight.shape[0]
    pooling = lookups // (grad_pooled.shape[0] * grad_pooled.shape[1])
    shards = lax.axis_size("shard")
    capacity = (3 * lookups + 2 * shards - 1) // (2 * shards)
    bags = grad_pooled.reshape(-1, width).astype(f32)
    rows = (bags[:, None, :] * lookup_weight.reshape(-1, pooling, 1)).reshape(lookups, width)
    rows = rows.astype(bf16)
    target_shard = owner[:, 0]
    hits = (target_shard[:, None] == jnp.arange(shards, dtype=i32)[None, :]).astype(i32)
    ranks = jnp.sum(jnp.cumsum(hits, axis=0) * hits, axis=1) - 1
    slots = target_shard * capacity + ranks
    outgoing = jnp.zeros((shards * capacity, width), bf16).at[slots].set(rows)
    row_ids = jnp.full((shards * capacity,), -1, i32).at[slots].set(local_row)
    received, received_ids = (
        lax.all_to_all(outgoing.reshape(shards, capacity, width), "shard", split_axis=0, concat_axis=0, tiled=True),
        lax.all_to_all(row_ids.reshape(shards, capacity), "shard", split_axis=0, concat_axis=0, tiled=True),
    )
    flat_rows = received.reshape(-1, width)
    flat_ids = received_ids.reshape(-1)
    window_rows = weight.shape[0]
    span = 512
    starts = jnp.arange(window_rows // span, dtype=i32) * span

    def one_block(start):
        shifted = flat_ids - start
        onehot = (jnp.arange(span, dtype=i32)[:, None] == shifted[None, :]).astype(bf16)
        return jnp.dot(onehot, flat_rows, preferred_element_type=f32)

    partial_grad = lax.map(one_block, starts).reshape(window_rows, width)
    table_grad = lax.psum(partial_grad, "rep")
    return adagrad(weight, accum, table_grad)


def iota(shape, dim, dtype=i32):
    return lax.broadcasted_iota(i32, shape, dim).astype(dtype)


def pack_kernel(groups, capacity, key_ref, owner_ref, row_ref, w_ref, bags_ref, keep_ref, give_ref, ext_ref):
    blocks = owner_ref.shape[0]
    wide = groups * blocks
    group = owner_ref[...] ^ key_ref[0]
    hits = [(group == g).astype(f32) for g in range(groups)]
    stacked = jnp.concatenate(hits, axis=0).astype(bf16)
    upper = (iota((LANES, LANES), 0) <= iota((LANES, LANES), 1)).astype(bf16)
    inside = jnp.dot(stacked, upper, preferred_element_type=f32)
    totals = jnp.dot(stacked, jnp.ones((LANES, LANES), bf16), preferred_element_type=f32)
    at, to = iota((wide, wide), 0), iota((wide, wide), 1)
    earlier = ((at // blocks == to // blocks) & (to < at)).astype(bf16)
    carry = jnp.dot(earlier, totals.astype(bf16), preferred_element_type=f32)
    rank = inside + carry - 1.0
    slot = jnp.zeros((blocks, LANES), f32)
    for g in range(groups):
        slot = slot + hits[g] * (rank[g * blocks:(g + 1) * blocks] + float(g * capacity))

    digits = jnp.concatenate(
        [(row_ref[...] >> 8).astype(f32), (row_ref[...] & 255).astype(f32), w_ref[...]]
        + [jnp.zeros((LANES - 3 * blocks, LANES), f32)], axis=0)
    columns = digits.T
    lane = iota((LANES, LANES), 1)
    repeat = ((iota((LANES, LANES // 2), 0) >> 1) == iota((LANES, LANES // 2), 1)).astype(bf16)
    for r in range(blocks):
        bag = jnp.dot(repeat, bags_ref[r * LANES // 2:(r + 1) * LANES // 2, :], preferred_element_type=f32)
        here = slice(r * LANES, (r + 1) * LANES)
        ext_ref[here, 0:LANES] = (bag * columns[:, 2 * blocks + r:2 * blocks + r + 1]).astype(bf16)
        high, low = columns[:, r:r + 1], columns[:, blocks + r:blocks + r + 1]
        ext_ref[here, LANES:2 * LANES] = jnp.where(
            lane == 0, high, jnp.where(lane == 1, low, 0.0)).astype(bf16)

    place = iota((LANES, LANES), 0, f32)
    chunks = capacity // LANES
    for turn in range(groups):
        g = (2 * (turn % (groups // 2)) + 1) if turn < groups // 2 else 2 * (turn - groups // 2)
        out_ref = give_ref if g % 2 else keep_ref
        high, low = [], []
        for k in range(chunks):
            moved = slot - float(g * capacity + k * LANES)
            picks = jnp.concatenate(
                [(place == moved[r:r + 1, :]).astype(bf16) for r in range(blocks)], axis=1)
            packed = jnp.dot(picks, ext_ref[...], preferred_element_type=f32)
            out_ref[g // 2, k * LANES:(k + 1) * LANES, :] = packed[:, :LANES].astype(bf16)
            turned = packed[:, LANES:].T
            high.append(turned[0:1])
            low.append(turned[1:2])
        out_ref[g // 2, capacity:capacity + PAD, :] = jnp.concatenate(
            high + low + [jnp.zeros((PAD - 2 * chunks, LANES), f32)], axis=0).astype(bf16)


def pack(key, owner, local_row, lookup_weight, bags, groups, capacity):
    blocks = owner.shape[0] // LANES
    shape = jax.ShapeDtypeStruct((groups // 2, capacity + PAD, LANES), bf16)
    vmem = pl.BlockSpec(memory_space=pltpu.VMEM)
    return pl.pallas_call(
        functools.partial(pack_kernel, groups, capacity),
        out_shape=[shape, shape],
        in_specs=[pl.BlockSpec(memory_space=pltpu.SMEM), vmem, vmem, vmem, vmem],
        out_specs=[vmem, vmem],
        scratch_shapes=[pltpu.VMEM((blocks * LANES, 2 * LANES), bf16)],
        compiler_params=pltpu.CompilerParams(vmem_limit_bytes=VMEM_LIMIT),
        name="pack",
    )(key, owner.reshape(blocks, LANES), local_row.reshape(blocks, LANES),
      lookup_weight.reshape(blocks, LANES), bags)


def add_kernel(capacity, lists, first, core_ref, *refs):
    in_refs, refs = refs[:lists], refs[lists:]
    before, (keep_ref, give_ref, rhs_ref) = (None, refs) if first else (refs[:2], refs[2:])
    half = keep_ref.shape[0]
    chunks = capacity // LANES
    highs, lows = [], []
    at = 0
    for ref in in_refs:
        for part in range(2):
            base = part * (capacity + PAD)
            digits = ref[base + capacity:base + capacity + PAD, :].astype(f32)
            high = digits[0:chunks]
            upper = (high >= float(half // 256)).astype(f32)
            give = jnp.where(core_ref[0] == 0, upper, 1.0 - upper)
            highs += [high[k:k + 1] - upper[k:k + 1] * float(half // 256) for k in range(chunks)]
            lows += [digits[chunks + k:chunks + k + 1] for k in range(chunks)]
            turned = jnp.concatenate([give, jnp.zeros((LANES - chunks, LANES), f32)], axis=0).T
            for k in range(chunks):
                rows = ref[base + k * LANES:base + (k + 1) * LANES, :].astype(f32)
                given = turned[:, k:k + 1] > 0.5
                here = slice(at, at + LANES)
                rhs_ref[here, 0:LANES] = jnp.where(given, 0.0, rows).astype(bf16)
                rhs_ref[here, LANES:2 * LANES] = jnp.where(given, rows, 0.0).astype(bf16)
                at += LANES
    place = iota((256, LANES), 0, f32)
    for h in range(half // 256):
        picks = jnp.concatenate(
            [(place == jnp.where(hi == float(h), lo, -1.0)).astype(bf16) for hi, lo in zip(highs, lows)], axis=1)
        part = jnp.dot(picks, rhs_ref[...], preferred_element_type=f32)
        here = slice(h * 256, (h + 1) * 256)
        keep, give = part[:, :LANES], part[:, LANES:]
        if before is not None:
            keep, give = keep + before[0][here, :], give + before[1][here, :]
        keep_ref[here, :] = keep
        give_ref[here, :] = give


def add_lists(core, lists, before, half, capacity):
    shape = jax.ShapeDtypeStruct((half, LANES), f32)
    vmem = pl.BlockSpec(memory_space=pltpu.VMEM)
    n = len(lists)
    depth = n * 2 * capacity
    return pl.pallas_call(
        functools.partial(add_kernel, capacity, n, before is None),
        out_shape=[shape, shape],
        in_specs=[pl.BlockSpec(memory_space=pltpu.SMEM)] + [vmem] * (n + (0 if before is None else 2)),
        out_specs=[vmem, vmem],
        scratch_shapes=[pltpu.VMEM((depth, 2 * LANES), bf16)],
        input_output_aliases={} if before is None else {n + 1: 0, n + 2: 1},
        compiler_params=pltpu.CompilerParams(vmem_limit_bytes=VMEM_LIMIT),
        cost_estimate=pl.CostEstimate(flops=4 * half * depth * LANES, bytes_accessed=4 * half * LANES * 4, transcendentals=0),
        name="add_lists",
    )(core, *lists, *([] if before is None else before))


def update_kernel(steps, core_ref, own_ref, own_y_ref, other_ref, other_y_ref, weight_ref, accum_ref,
                  new_weight_ref, new_accum_ref, columns_ref, sums_ref):
    step = pl.program_id(0)
    blocks = accum_ref.shape[0]
    span = weight_ref.shape[0]

    @pl.when(step == 0)
    def _():
        columns_ref[...] = jnp.concatenate(
            [accum_ref[...], jnp.zeros((LANES - blocks, LANES), f32)], axis=0).T
        sums_ref[...] = jnp.zeros((LANES, LANES), f32)

    mine = (step >= steps // 2) == (core_ref[0] == 1)
    lane = iota((LANES, LANES), 1)
    start = (step % (steps // 2)) * span
    for k in range(span // LANES):
        at = pl.ds(pl.multiple_of(start + k * LANES, LANES), LANES)
        here = slice(k * LANES, (k + 1) * LANES)
        near = own_ref[at, :].astype(f32) + own_y_ref[at, :].astype(f32)
        far = other_ref[at, :].astype(f32) + other_y_ref[at, :].astype(f32)
        grad = jnp.where(mine, near, far)
        hit = lane == step * (span // LANES) + k
        old = jnp.sum(jnp.where(hit, columns_ref[...], 0.0), axis=1, keepdims=True)
        new = old + jnp.sum(grad * grad, axis=1, keepdims=True) * (1.0 / LANES)
        sums_ref[...] = jnp.where(hit, new, sums_ref[...])
        new_weight_ref[here, :] = weight_ref[here, :] - grad * (step_size / (jnp.sqrt(new) + epsilon))

    @pl.when(step == steps - 1)
    def _():
        new_accum_ref[...] = sums_ref[...].T[:blocks]


def update(core, own, own_y, other, other_y, weight, accum):
    rows = weight.shape[0]
    blocks = rows // LANES
    steps = 8
    span = rows // steps
    whole = pl.BlockSpec(memory_space=pltpu.VMEM)
    new_weight, new_accum = pl.pallas_call(
        functools.partial(update_kernel, steps),
        grid=(steps,),
        out_shape=[jax.ShapeDtypeStruct(weight.shape, f32), jax.ShapeDtypeStruct((blocks, LANES), f32)],
        in_specs=[pl.BlockSpec(memory_space=pltpu.SMEM), whole, whole, whole, whole,
                  pl.BlockSpec((span, LANES), lambda i: (i, 0)), whole],
        out_specs=[pl.BlockSpec((span, LANES), lambda i: (i, 0)), pl.BlockSpec((blocks, LANES), lambda i: (0, 0))],
        scratch_shapes=[pltpu.VMEM((LANES, LANES), f32), pltpu.VMEM((LANES, LANES), f32)],
        compiler_params=pltpu.CompilerParams(vmem_limit_bytes=VMEM_LIMIT),
        name="update",
    )(core, own, own_y, other, other_y, weight, accum.reshape(blocks, LANES))
    return new_weight, new_accum.reshape(-1)


def paired_body(shards, reps, grad_pooled, lookup_weight, owner, local_row, weight, accum):
    width = grad_pooled.shape[-1]
    lookups = lookup_weight.shape[0]
    capacity = (3 * lookups + 2 * shards - 1) // (2 * shards)
    half = weight.shape[0] // 2
    axes = ("shard", "rep")

    def permute(value, target):
        pairs = [(s * reps + r, target(s, r)) for s in range(shards) for r in range(reps)]
        return lax.ppermute(value, axes, pairs)

    to_core = functools.partial(permute, target=lambda s, r: s * reps + (r ^ 1))
    to_copy = functools.partial(permute, target=lambda s, r: s * reps + (r ^ 2))
    core = (lax.axis_index("rep") & 1).astype(i32)
    key = (lax.axis_index("shard").astype(i32) ^ core).reshape(1)
    core = core.reshape(1)

    keep, give = pack(key, owner, local_row, lookup_weight, grad_pooled.reshape(-1, width), shards, capacity)
    got = to_core(give)
    arrived = {}
    for q in reversed(range(shards // 2)):
        arrived[q] = permute(jnp.concatenate([keep[q], got[q]], axis=0),
                             lambda s, r: (s ^ (2 * q + (r & 1))) * reps + r)
    near, far = range(shards // 4), range(shards // 4, shards // 2)
    sums = add_lists(core, [arrived[q] for q in near], None, half, capacity)
    for q in far:
        sums = add_lists(core, [arrived[q]], sums, half, capacity)
    mine, other = sums
    own = (mine + to_core(other)).astype(bf16)
    own_y = to_copy(own)
    return update(core, own, own_y, to_core(own), to_core(own_y), weight, accum)


def solution(mesh):
    shards, reps = mesh.shape["shard"], mesh.shape["rep"]
    in_specs = (
        P(("shard", "rep"), None, None),
        P(("shard", "rep")),
        P(("shard", "rep"), None),
        P(("shard", "rep")),
        P("shard", None),
        P("shard"),
    )
    out_specs = (P("shard", None), P("shard"))
    paired = reps == 4 and shards == 8
    body = functools.partial(paired_body, shards, reps) if paired else general_body
    return jax.shard_map(body, mesh=mesh, in_specs=in_specs, out_specs=out_specs, check_vma=False)
```

```python
import functools

import jax
import jax.numpy as jnp
from jax import lax
from jax.experimental import pallas as pl
from jax.experimental.pallas import tpu as pltpu
from jax.sharding import PartitionSpec as P

step_size = 0.25
epsilon = 1e-08
f32, bf16, i32 = jnp.float32, jnp.bfloat16, jnp.int32
LANES = 128
PAD = 16
VMEM_LIMIT = 48 * 1024 * 1024
MEDIUM = pl.CostEstimate(flops=100_000_000, bytes_accessed=1024, transcendentals=0)
SMALL = pl.CostEstimate(flops=1024, bytes_accessed=1024, transcendentals=0)


def adagrad(weight, accum, table_grad):
    new_accum = accum + jnp.mean(table_grad * table_grad, axis=1)
    new_weight = weight - step_size * table_grad / (jnp.sqrt(new_accum)[:, None] + epsilon)
    return (new_weight, new_accum)


def general_body(grad_pooled, lookup_weight, owner, local_row, weight, accum):
    width = grad_pooled.shape[-1]
    lookups = lookup_weight.shape[0]
    pooling = lookups // (grad_pooled.shape[0] * grad_pooled.shape[1])
    shards = lax.axis_size("shard")
    capacity = (3 * lookups + 2 * shards - 1) // (2 * shards)
    bags = grad_pooled.reshape(-1, width).astype(f32)
    rows = (bags[:, None, :] * lookup_weight.reshape(-1, pooling, 1)).reshape(lookups, width)
    rows = rows.astype(bf16)
    target_shard = owner[:, 0]
    hits = (target_shard[:, None] == jnp.arange(shards, dtype=i32)[None, :]).astype(i32)
    ranks = jnp.sum(jnp.cumsum(hits, axis=0) * hits, axis=1) - 1
    slots = target_shard * capacity + ranks
    outgoing = jnp.zeros((shards * capacity, width), bf16).at[slots].set(rows)
    row_ids = jnp.full((shards * capacity,), -1, i32).at[slots].set(local_row)
    received, received_ids = (
        lax.all_to_all(outgoing.reshape(shards, capacity, width), "shard", split_axis=0, concat_axis=0, tiled=True),
        lax.all_to_all(row_ids.reshape(shards, capacity), "shard", split_axis=0, concat_axis=0, tiled=True),
    )
    flat_rows = received.reshape(-1, width)
    flat_ids = received_ids.reshape(-1)
    window_rows = weight.shape[0]
    span = 512
    starts = jnp.arange(window_rows // span, dtype=i32) * span

    def one_block(start):
        shifted = flat_ids - start
        onehot = (jnp.arange(span, dtype=i32)[:, None] == shifted[None, :]).astype(bf16)
        return jnp.dot(onehot, flat_rows, preferred_element_type=f32)

    partial_grad = lax.map(one_block, starts).reshape(window_rows, width)
    table_grad = lax.psum(partial_grad, "rep")
    return adagrad(weight, accum, table_grad)


def iota(shape, dim, dtype=i32):
    return lax.broadcasted_iota(i32, shape, dim).astype(dtype)


def pack_groups(groups, capacity, wanted, slot, ext_ref, out_ref):
    blocks = slot.shape[0]
    chunks = capacity // LANES
    place = iota((LANES, LANES), 0, f32)
    for n, g in enumerate(wanted):
        high, low = [], []
        for k in range(chunks):
            moved = slot - float(g * capacity + k * LANES)
            picks = jnp.concatenate(
                [(place == moved[r:r + 1, :]).astype(bf16) for r in range(blocks)], axis=1)
            packed = jnp.dot(picks, ext_ref[...], preferred_element_type=f32)
            out_ref[n, k * LANES:(k + 1) * LANES, :] = packed[:, :LANES].astype(bf16)
            turned = packed[:, LANES:].T
            high.append(turned[0:1])
            low.append(turned[1:2])
        out_ref[n, capacity:capacity + PAD, :] = jnp.concatenate(
            high + low + [jnp.zeros((PAD - 2 * chunks, LANES), f32)], axis=0).astype(bf16)


def first_kernel(groups, capacity, wanted, facts_ref, bags_ref, out_ref, slot_ref, ext_ref):
    blocks = slot_ref.shape[0]
    wide = groups * blocks
    upper = (iota((LANES, LANES), 0) <= iota((LANES, LANES), 1)).astype(bf16)
    at, to = iota((wide, wide), 0), iota((wide, wide), 1)
    earlier = ((at // blocks == to // blocks) & (to < at)).astype(bf16)
    lane = iota((LANES, LANES), 1)
    repeat = ((iota((LANES, LANES // 2), 0) >> 1) == iota((LANES, LANES // 2), 1)).astype(bf16)
    group = facts_ref[0:blocks, :]
    hits = [(group == float(g)).astype(f32) for g in range(groups)]
    stacked = jnp.concatenate(hits, axis=0).astype(bf16)
    inside = jnp.dot(stacked, upper, preferred_element_type=f32)
    totals = jnp.dot(stacked, jnp.ones((LANES, LANES), bf16), preferred_element_type=f32)
    carry = jnp.dot(earlier, totals.astype(bf16), preferred_element_type=f32)
    rank = inside + carry - 1.0
    slot = jnp.zeros((blocks, LANES), f32)
    for g in range(groups):
        slot = slot + hits[g] * (rank[g * blocks:(g + 1) * blocks] + float(g * capacity))
    slot_ref[...] = slot

    columns = jnp.concatenate(
        [facts_ref[blocks:4 * blocks, :], jnp.zeros((LANES - 3 * blocks, LANES), f32)], axis=0).T
    for r in range(blocks):
        bag = jnp.dot(repeat, bags_ref[r * LANES // 2:(r + 1) * LANES // 2, :], preferred_element_type=f32)
        here = slice(r * LANES, (r + 1) * LANES)
        ext_ref[here, 0:LANES] = (bag * columns[:, 2 * blocks + r:2 * blocks + r + 1]).astype(bf16)
        high, low = columns[:, r:r + 1], columns[:, blocks + r:blocks + r + 1]
        ext_ref[here, LANES:2 * LANES] = jnp.where(
            lane == 0, high, jnp.where(lane == 1, low, 0.0)).astype(bf16)
    pack_groups(groups, capacity, wanted, slot, ext_ref, out_ref)


def next_kernel(groups, capacity, wanted, slot_ref, ext_ref, *refs):
    out_ref = refs[-1]
    pack_groups(groups, capacity, wanted, slot_ref[...], ext_ref, out_ref)


def listed(wanted, capacity):
    return jax.ShapeDtypeStruct((len(wanted), capacity + PAD, LANES), bf16)


def pack_first(facts, bags, groups, capacity, wanted):
    blocks = facts.shape[0] // 4
    vmem = pl.BlockSpec(memory_space=pltpu.VMEM)
    return pl.pallas_call(
        functools.partial(first_kernel, groups, capacity, wanted),
        out_shape=[listed(wanted, capacity), jax.ShapeDtypeStruct((blocks, LANES), f32),
                   jax.ShapeDtypeStruct((blocks * LANES, 2 * LANES), bf16)],
        in_specs=[vmem, vmem],
        out_specs=[vmem, vmem, vmem],
        compiler_params=pltpu.CompilerParams(vmem_limit_bytes=VMEM_LIMIT),
        name="pack_first",
    )(facts, bags)


def pack_next(slot, ext, groups, capacity, wanted, after=()):
    vmem = pl.BlockSpec(memory_space=pltpu.VMEM)
    return pl.pallas_call(
        functools.partial(next_kernel, groups, capacity, wanted),
        out_shape=listed(wanted, capacity),
        in_specs=[vmem, vmem] + [pl.BlockSpec(memory_space=pl.ANY)] * len(after),
        out_specs=vmem,
        compiler_params=pltpu.CompilerParams(vmem_limit_bytes=VMEM_LIMIT),
        cost_estimate=SMALL,
        name="pack_next",
    )(slot, ext, *after)


def add_kernel(capacity, lists, first, last, *refs):
    in_refs, refs = refs[:lists], list(refs[lists:])
    before = None if first else refs.pop(0)
    beside = refs.pop(0) if last else None
    out_ref, rhs_ref = refs
    half = out_ref.shape[0]
    chunks = capacity // LANES
    highs, lows = [], []
    at = 0
    for ref in in_refs:
        for part in range(ref.shape[0] // (capacity + PAD)):
            base = part * (capacity + PAD)
            digits = ref[base + capacity:base + capacity + PAD, :].astype(f32)
            high = digits[0:chunks]
            upper = (high >= float(half // 256)).astype(f32)
            high = high - upper * float(half // 256)
            highs += [high[k:k + 1] for k in range(chunks)]
            lows += [digits[chunks + k:chunks + k + 1] for k in range(chunks)]
            turned = jnp.concatenate([upper, jnp.zeros((LANES - chunks, LANES), f32)], axis=0).T
            for k in range(chunks):
                rows = ref[base + k * LANES:base + (k + 1) * LANES, :].astype(f32)
                above = turned[:, k:k + 1] > 0.5
                here = slice(at, at + LANES)
                rhs_ref[here, 0:LANES] = jnp.where(above, 0.0, rows).astype(bf16)
                rhs_ref[here, LANES:2 * LANES] = jnp.where(above, rows, 0.0).astype(bf16)
                at += LANES
    place = iota((256, LANES), 0, f32)
    for h in range(half // 256):
        picks = jnp.concatenate(
            [(place == jnp.where(hi == float(h), lo, -1.0)).astype(bf16) for hi, lo in zip(highs, lows)], axis=1)
        part = jnp.dot(picks, rhs_ref[...], preferred_element_type=f32)
        here = slice(h * 256, (h + 1) * 256)
        if before is not None:
            part = part + before[here, :]
        if beside is not None:
            part = part + beside[here, :]
        out_ref[here, :] = part.astype(out_ref.dtype)


def add_lists(lists, before, beside, half, capacity):
    vmem = pl.BlockSpec(memory_space=pltpu.VMEM)
    n = len(lists)
    depth = sum(value.shape[0] for value in lists) // (capacity + PAD) * capacity
    more = [value for value in (before, beside) if value is not None]
    return pl.pallas_call(
        functools.partial(add_kernel, capacity, n, before is None, beside is not None),
        out_shape=jax.ShapeDtypeStruct((half, 2 * LANES), f32 if beside is None else bf16),
        in_specs=[vmem] * (n + len(more)),
        out_specs=vmem,
        scratch_shapes=[pltpu.VMEM((depth, 2 * LANES), bf16)],
        input_output_aliases={n: 0} if beside is None and before is not None else {},
        compiler_params=pltpu.CompilerParams(vmem_limit_bytes=VMEM_LIMIT),
        cost_estimate=MEDIUM,
        name="add_lists",
    )(*lists, *more)


def update_kernel(own_ref, other_ref, weight_ref, accum_ref, new_weight_hbm, new_accum_ref, out_ref, sems):
    blocks = accum_ref.shape[0]
    half = own_ref.shape[0]
    parts = 4
    span = blocks // parts
    lane = iota((LANES, LANES), 1)

    def grad(b):
        top = (b * LANES) % half
        side = (b * LANES) // half
        at, to = slice(top, top + LANES), slice(side * LANES, (side + 1) * LANES)
        return own_ref[at, to].astype(f32) + other_ref[at, to].astype(f32)

    old = jnp.concatenate([accum_ref[...], jnp.zeros((LANES - blocks, LANES), f32)], axis=0).T
    new = old
    copies = []
    for p in range(parts):
        for b in range(p * span, (p + 1) * span):
            g = grad(b)
            new = jnp.where(lane == b, new + jnp.sum(g * g, axis=1, keepdims=True) * (1.0 / LANES), new)
        scale = step_size / (jnp.sqrt(new) + epsilon)
        for b in range(p * span, (p + 1) * span):
            here = slice(b * LANES, (b + 1) * LANES)
            out_ref[here, :] = weight_ref[here, :] - grad(b) * scale[:, b:b + 1]
        rows = slice(p * span * LANES, (p + 1) * span * LANES)
        copies.append(pltpu.make_async_copy(out_ref.at[rows], new_weight_hbm.at[rows], sems.at[p]))
        copies[-1].start()
    new_accum_ref[...] = new.T[:blocks]
    for copy in copies:
        copy.wait()


def update(own, other, weight, accum):
    rows = weight.shape[0]
    blocks = rows // LANES
    vmem, hbm = pl.BlockSpec(memory_space=pltpu.VMEM), pl.BlockSpec(memory_space=pltpu.HBM)
    new_weight, new_accum = pl.pallas_call(
        update_kernel,
        out_shape=[jax.ShapeDtypeStruct(weight.shape, f32), jax.ShapeDtypeStruct((blocks, LANES), f32)],
        in_specs=[vmem, vmem, vmem, vmem],
        out_specs=[hbm, vmem],
        scratch_shapes=[pltpu.VMEM(weight.shape, f32), pltpu.SemaphoreType.DMA((4,))],
        compiler_params=pltpu.CompilerParams(vmem_limit_bytes=VMEM_LIMIT),
        name="update",
    )(own, other, weight, accum.reshape(blocks, LANES))
    return new_weight, new_accum.reshape(-1)


def tied(value, after):
    return value + (after[-1:, 0:LANES] * 0.0).astype(value.dtype)


def paired_body(shards, reps, grad_pooled, lookup_weight, owner, local_row, weight, accum):
    width = grad_pooled.shape[-1]
    lookups = lookup_weight.shape[0]
    capacity = (3 * lookups + 2 * shards - 1) // (2 * shards)
    half = weight.shape[0] // 2
    axes = ("shard", "rep")

    def permute(value, target):
        pairs = [(s * reps + r, target(s, r)) for s in range(shards) for r in range(reps)]
        return lax.ppermute(value, axes, pairs)

    to_core = functools.partial(permute, target=lambda s, r: s * reps + (r ^ 1))
    to_copy = functools.partial(permute, target=lambda s, r: s * reps + (r ^ 2))
    key = lax.axis_index("shard").astype(i32) ^ (lax.axis_index("rep").astype(i32) & 1)
    blocks = lookups // LANES
    local_row = local_row.reshape(blocks, LANES)
    facts = jnp.concatenate(
        [(owner.reshape(blocks, LANES) ^ key).astype(f32), (local_row >> 8).astype(f32),
         (local_row & 255).astype(f32), lookup_weight.reshape(blocks, LANES)], axis=0)

    near = list(range(shards // 4))
    far = list(range(shards // 4, shards // 2))
    phases = [far[1:], near + far[:1]]
    order = [near, far[1:], far[:1]]
    before, arrived = (), {}
    for n, qs in enumerate(phases):
        give, hold = [2 * q + 1 for q in qs], [2 * q for q in qs]
        if n == 0:
            given, slot, ext = pack_first(facts, grad_pooled.reshape(-1, width), shards, capacity, give)
        else:
            given = pack_next(slot, ext, shards, capacity, give, before)
        got = to_core(given)
        keep = pack_next(slot, ext, shards, capacity, hold, before)
        before = [jnp.concatenate([keep[n], got[n]], axis=0) for n in range(len(qs))]
        for q, payload in zip(qs, before):
            arrived[q] = permute(payload, lambda s, r: (s ^ (2 * q + (r & 1))) * reps + r)

    own = copy = None
    for n, qs in enumerate(order):
        here = jnp.concatenate([arrived[q] for q in qs], axis=0)
        if own is not None:
            here = tied(here, own)
        there = to_copy(here)
        own = add_lists([here], own, None, half, capacity)
        copy = add_lists([there], copy, own if n == 2 else None, half, capacity)
    return update(copy, to_core(copy), weight, accum)


def solution(mesh):
    shards, reps = mesh.shape["shard"], mesh.shape["rep"]
    in_specs = (
        P(("shard", "rep"), None, None),
        P(("shard", "rep")),
        P(("shard", "rep"), None),
        P(("shard", "rep")),
        P("shard", None),
        P("shard"),
    )
    out_specs = (P("shard", None), P("shard"))
    paired = reps == 4 and shards == 8
    body = functools.partial(paired_body, shards, reps) if paired else general_body
    return jax.shard_map(body, mesh=mesh, in_specs=in_specs, out_specs=out_specs, check_vma=False)
```

```python
import functools

import jax
import jax.numpy as jnp
from jax import lax
from jax.experimental import pallas as pl
from jax.experimental.pallas import tpu as pltpu
from jax.sharding import PartitionSpec as P

step_size = 0.25
epsilon = 1e-08
f32, bf16, i32 = jnp.float32, jnp.bfloat16, jnp.int32
LANES = 128
PAD = 16
VMEM_LIMIT = 48 * 1024 * 1024
MEDIUM = pl.CostEstimate(flops=100_000_000, bytes_accessed=1024, transcendentals=0)
SMALL = pl.CostEstimate(flops=1024, bytes_accessed=1024, transcendentals=0)


def adagrad(weight, accum, table_grad):
    new_accum = accum + jnp.mean(table_grad * table_grad, axis=1)
    new_weight = weight - step_size * table_grad / (jnp.sqrt(new_accum)[:, None] + epsilon)
    return (new_weight, new_accum)


def general_body(grad_pooled, lookup_weight, owner, local_row, weight, accum):
    width = grad_pooled.shape[-1]
    lookups = lookup_weight.shape[0]
    pooling = lookups // (grad_pooled.shape[0] * grad_pooled.shape[1])
    shards = lax.axis_size("shard")
    capacity = (3 * lookups + 2 * shards - 1) // (2 * shards)
    bags = grad_pooled.reshape(-1, width).astype(f32)
    rows = (bags[:, None, :] * lookup_weight.reshape(-1, pooling, 1)).reshape(lookups, width)
    rows = rows.astype(bf16)
    target_shard = owner[:, 0]
    hits = (target_shard[:, None] == jnp.arange(shards, dtype=i32)[None, :]).astype(i32)
    ranks = jnp.sum(jnp.cumsum(hits, axis=0) * hits, axis=1) - 1
    slots = target_shard * capacity + ranks
    outgoing = jnp.zeros((shards * capacity, width), bf16).at[slots].set(rows)
    row_ids = jnp.full((shards * capacity,), -1, i32).at[slots].set(local_row)
    received, received_ids = (
        lax.all_to_all(outgoing.reshape(shards, capacity, width), "shard", split_axis=0, concat_axis=0, tiled=True),
        lax.all_to_all(row_ids.reshape(shards, capacity), "shard", split_axis=0, concat_axis=0, tiled=True),
    )
    flat_rows = received.reshape(-1, width)
    flat_ids = received_ids.reshape(-1)
    window_rows = weight.shape[0]
    span = 512
    starts = jnp.arange(window_rows // span, dtype=i32) * span

    def one_block(start):
        shifted = flat_ids - start
        onehot = (jnp.arange(span, dtype=i32)[:, None] == shifted[None, :]).astype(bf16)
        return jnp.dot(onehot, flat_rows, preferred_element_type=f32)

    partial_grad = lax.map(one_block, starts).reshape(window_rows, width)
    table_grad = lax.psum(partial_grad, "rep")
    return adagrad(weight, accum, table_grad)


def iota(shape, dim, dtype=i32):
    return lax.broadcasted_iota(i32, shape, dim).astype(dtype)


def pack_groups(groups, capacity, wanted, slot, ext_ref, out_ref):
    blocks = slot.shape[0]
    chunks = capacity // LANES
    place = iota((LANES, LANES), 0, f32)
    for n, g in enumerate(wanted):
        high, low = [], []
        for k in range(chunks):
            moved = slot - float(g * capacity + k * LANES)
            picks = jnp.concatenate(
                [(place == moved[r:r + 1, :]).astype(bf16) for r in range(blocks)], axis=1)
            packed = jnp.dot(picks, ext_ref[...], preferred_element_type=f32)
            out_ref[n, k * LANES:(k + 1) * LANES, :] = packed[:, :LANES].astype(bf16)
            turned = packed[:, LANES:].T
            high.append(turned[0:1])
            low.append(turned[1:2])
        out_ref[n, capacity:capacity + PAD, :] = jnp.concatenate(
            high + low + [jnp.zeros((PAD - 2 * chunks, LANES), f32)], axis=0).astype(bf16)


def rank_kernel(groups, capacity, code_ref, owner_ref, slot_ref):
    blocks = slot_ref.shape[0]
    wide = groups * blocks
    upper = (iota((LANES, LANES), 0) <= iota((LANES, LANES), 1)).astype(bf16)
    at, to = iota((wide, wide), 0), iota((wide, wide), 1)
    earlier = ((at // blocks == to // blocks) & (to < at)).astype(bf16)
    offset = owner_ref[...] ^ (code_ref[0] >> 1)
    group = jnp.where(offset < 2, offset, offset ^ (code_ref[0] & 1))
    hits = [(group == g).astype(f32) for g in range(groups)]
    stacked = jnp.concatenate(hits, axis=0).astype(bf16)
    inside = jnp.dot(stacked, upper, preferred_element_type=f32)
    totals = jnp.dot(stacked, jnp.ones((LANES, LANES), bf16), preferred_element_type=f32)
    carry = jnp.dot(earlier, totals.astype(bf16), preferred_element_type=f32)
    rank = inside + carry - 1.0
    slot = jnp.zeros((blocks, LANES), f32)
    for g in range(groups):
        slot = slot + hits[g] * (rank[g * blocks:(g + 1) * blocks] + float(g * capacity))
    slot_ref[...] = slot


def first_kernel(groups, capacity, wanted, slot_ref, row_ref, w_ref, bags_ref, out_ref, ext_ref):
    blocks = slot_ref.shape[0]
    lane = iota((LANES, LANES), 1)
    repeat = ((iota((LANES, LANES // 2), 0) >> 1) == iota((LANES, LANES // 2), 1)).astype(bf16)
    columns = jnp.concatenate(
        [(row_ref[...] >> 8).astype(f32), (row_ref[...] & 255).astype(f32), w_ref[...],
         jnp.zeros((LANES - 3 * blocks, LANES), f32)], axis=0).T
    for r in range(blocks):
        bag = jnp.dot(repeat, bags_ref[r * LANES // 2:(r + 1) * LANES // 2, :], preferred_element_type=f32)
        here = slice(r * LANES, (r + 1) * LANES)
        ext_ref[here, 0:LANES] = (bag * columns[:, 2 * blocks + r:2 * blocks + r + 1]).astype(bf16)
        high, low = columns[:, r:r + 1], columns[:, blocks + r:blocks + r + 1]
        ext_ref[here, LANES:2 * LANES] = jnp.where(
            lane == 0, high, jnp.where(lane == 1, low, 0.0)).astype(bf16)
    pack_groups(groups, capacity, wanted, slot_ref[...], ext_ref, out_ref)


def next_kernel(groups, capacity, wanted, slot_ref, ext_ref, *refs):
    out_ref = refs[-1]
    pack_groups(groups, capacity, wanted, slot_ref[...], ext_ref, out_ref)


def listed(wanted, capacity):
    return jax.ShapeDtypeStruct((len(wanted), capacity + PAD, LANES), bf16)


def find_slots(code, owner, groups, capacity):
    vmem = pl.BlockSpec(memory_space=pltpu.VMEM)
    return pl.pallas_call(
        functools.partial(rank_kernel, groups, capacity),
        out_shape=jax.ShapeDtypeStruct(owner.shape, f32),
        in_specs=[pl.BlockSpec(memory_space=pltpu.SMEM), vmem],
        out_specs=vmem,
        compiler_params=pltpu.CompilerParams(vmem_limit_bytes=VMEM_LIMIT),
        cost_estimate=pl.CostEstimate(flops=20_000_000_000, bytes_accessed=1024, transcendentals=0),
        name="find_slots",
    )(code, owner)


def pack_first(slot, local_row, lookup_weight, bags, groups, capacity, wanted):
    vmem = pl.BlockSpec(memory_space=pltpu.VMEM)
    return pl.pallas_call(
        functools.partial(first_kernel, groups, capacity, wanted),
        out_shape=[listed(wanted, capacity), jax.ShapeDtypeStruct((slot.size, 2 * LANES), bf16)],
        in_specs=[vmem] * 4,
        out_specs=[vmem, vmem],
        compiler_params=pltpu.CompilerParams(vmem_limit_bytes=VMEM_LIMIT),
        name="pack_first",
    )(slot, local_row, lookup_weight, bags)


def pack_next(slot, ext, groups, capacity, wanted, after=()):
    vmem = pl.BlockSpec(memory_space=pltpu.VMEM)
    return pl.pallas_call(
        functools.partial(next_kernel, groups, capacity, wanted),
        out_shape=listed(wanted, capacity),
        in_specs=[vmem, vmem] + [pl.BlockSpec(memory_space=pl.ANY)] * len(after),
        out_specs=vmem,
        compiler_params=pltpu.CompilerParams(vmem_limit_bytes=VMEM_LIMIT),
        cost_estimate=SMALL,
        name="pack_next",
    )(slot, ext, *after)


def add_kernel(capacity, lists, first, last, *refs):
    in_refs, refs = refs[:lists], list(refs[lists:])
    before = None if first else refs.pop(0)
    beside = refs.pop(0) if last else None
    out_ref, rhs_ref = refs
    half = out_ref.shape[0]
    chunks = capacity // LANES
    highs, lows = [], []
    at = 0
    for ref in in_refs:
        for part in range(ref.shape[0] // (capacity + PAD)):
            base = part * (capacity + PAD)
            digits = ref[base + capacity:base + capacity + PAD, :].astype(f32)
            high = digits[0:chunks]
            upper = (high >= float(half // 256)).astype(f32)
            high = high - upper * float(half // 256)
            highs += [high[k:k + 1] for k in range(chunks)]
            lows += [digits[chunks + k:chunks + k + 1] for k in range(chunks)]
            turned = jnp.concatenate([upper, jnp.zeros((LANES - chunks, LANES), f32)], axis=0).T
            for k in range(chunks):
                rows = ref[base + k * LANES:base + (k + 1) * LANES, :].astype(f32)
                above = turned[:, k:k + 1] > 0.5
                here = slice(at, at + LANES)
                rhs_ref[here, 0:LANES] = jnp.where(above, 0.0, rows).astype(bf16)
                rhs_ref[here, LANES:2 * LANES] = jnp.where(above, rows, 0.0).astype(bf16)
                at += LANES
    place = iota((256, LANES), 0, f32)
    for h in range(half // 256):
        picks = jnp.concatenate(
            [(place == jnp.where(hi == float(h), lo, -1.0)).astype(bf16) for hi, lo in zip(highs, lows)], axis=1)
        part = jnp.dot(picks, rhs_ref[...], preferred_element_type=f32)
        here = slice(h * 256, (h + 1) * 256)
        if before is not None:
            part = part + before[here, :]
        if beside is not None:
            part = part + beside[here, :]
        out_ref[here, :] = part.astype(out_ref.dtype)


def add_lists(lists, before, beside, half, capacity):
    vmem = pl.BlockSpec(memory_space=pltpu.VMEM)
    n = len(lists)
    depth = sum(value.shape[0] for value in lists) // (capacity + PAD) * capacity
    more = [value for value in (before, beside) if value is not None]
    return pl.pallas_call(
        functools.partial(add_kernel, capacity, n, before is None, beside is not None),
        out_shape=jax.ShapeDtypeStruct((half, 2 * LANES), f32 if beside is None else bf16),
        in_specs=[vmem] * (n + len(more)),
        out_specs=vmem,
        scratch_shapes=[pltpu.VMEM((depth, 2 * LANES), bf16)],
        input_output_aliases={n: 0} if beside is None and before is not None else {},
        compiler_params=pltpu.CompilerParams(vmem_limit_bytes=VMEM_LIMIT),
        cost_estimate=MEDIUM,
        name="add_lists",
    )(*lists, *more)


def update_kernel(own_ref, other_ref, weight_ref, accum_ref, new_weight_hbm, new_accum_ref, out_ref, sems):
    blocks = accum_ref.shape[0]
    half = own_ref.shape[0]
    parts = 4
    span = blocks // parts
    lane = iota((LANES, LANES), 1)

    def grad(b):
        top = (b * LANES) % half
        side = (b * LANES) // half
        at, to = slice(top, top + LANES), slice(side * LANES, (side + 1) * LANES)
        return own_ref[at, to].astype(f32) + other_ref[at, to].astype(f32)

    old = jnp.concatenate([accum_ref[...], jnp.zeros((LANES - blocks, LANES), f32)], axis=0).T
    new = old
    copies = []
    for p in range(parts):
        for b in range(p * span, (p + 1) * span):
            g = grad(b)
            new = jnp.where(lane == b, new + jnp.sum(g * g, axis=1, keepdims=True) * (1.0 / LANES), new)
        scale = step_size / (jnp.sqrt(new) + epsilon)
        for b in range(p * span, (p + 1) * span):
            here = slice(b * LANES, (b + 1) * LANES)
            out_ref[here, :] = weight_ref[here, :] - grad(b) * scale[:, b:b + 1]
        rows = slice(p * span * LANES, (p + 1) * span * LANES)
        copies.append(pltpu.make_async_copy(out_ref.at[rows], new_weight_hbm.at[rows], sems.at[p]))
        copies[-1].start()
    new_accum_ref[...] = new.T[:blocks]
    for copy in copies:
        copy.wait()


def update(own, other, weight, accum):
    rows = weight.shape[0]
    blocks = rows // LANES
    vmem, hbm = pl.BlockSpec(memory_space=pltpu.VMEM), pl.BlockSpec(memory_space=pltpu.HBM)
    new_weight, new_accum = pl.pallas_call(
        update_kernel,
        out_shape=[jax.ShapeDtypeStruct(weight.shape, f32), jax.ShapeDtypeStruct((blocks, LANES), f32)],
        in_specs=[vmem, vmem, vmem, vmem],
        out_specs=[hbm, vmem],
        scratch_shapes=[pltpu.VMEM(weight.shape, f32), pltpu.SemaphoreType.DMA((4,))],
        compiler_params=pltpu.CompilerParams(vmem_limit_bytes=VMEM_LIMIT),
        name="update",
    )(own, other, weight, accum.reshape(blocks, LANES))
    return new_weight, new_accum.reshape(-1)


def tied(value, after):
    return value + (after[-1:, 0:LANES] * 0.0).astype(value.dtype)


def paired_body(shards, reps, grad_pooled, lookup_weight, owner, local_row, weight, accum):
    width = grad_pooled.shape[-1]
    lookups = lookup_weight.shape[0]
    capacity = (3 * lookups + 2 * shards - 1) // (2 * shards)
    half = weight.shape[0] // 2
    axes = ("shard", "rep")

    def permute(value, target):
        pairs = [(s * reps + r, target(s, r)) for s in range(shards) for r in range(reps)]
        return lax.ppermute(value, axes, pairs)

    to_core = functools.partial(permute, target=lambda s, r: s * reps + (r ^ 1))
    to_copy = functools.partial(permute, target=lambda s, r: s * reps + (r ^ 2))
    code = lax.axis_index("shard").astype(i32) * 2 + (lax.axis_index("rep").astype(i32) & 1)
    dense = (lookups // LANES, LANES)
    slot = find_slots(code.reshape(1), owner.reshape(dense), shards, capacity)

    def swapped(qs, pack_given, after):
        got = to_core(pack_given)
        keep = pack_next(slot, ext, shards, capacity, [2 * q for q in qs], after)
        return [jnp.concatenate([keep[n], got[n]], axis=0) for n in range(len(qs))]

    def send(q, payload):
        return permute(payload, lambda s, r: (s ^ (2 * q + (r & 1))) * reps + r)

    far = shards // 2 - 1
    near = [1, far - 1]
    given, ext = pack_first(slot, local_row.reshape(dense), lookup_weight.reshape(dense),
                            grad_pooled.reshape(-1, width), shards, capacity, [2 * far + 1])
    first = swapped([far], given, ())
    lists = {far: send(far, first[0])}
    given = pack_next(slot, ext, shards, capacity, [2 * q + 1 for q in near], first)
    got = to_core(given)
    kept = pack_next(slot, ext, shards, capacity, [2 * q for q in near], first)
    beside = pack_next(slot, ext, shards, capacity, [0, 1], [got])
    lists[0] = jnp.concatenate([beside[0], permute(beside[1], lambda s, r: (s ^ 1) * reps + r)], axis=0)
    for n, q in enumerate(near):
        lists[q] = send(q, jnp.concatenate([kept[n], got[n]], axis=0))

    own = copy = None
    order = (0, far, 1, far - 1)
    for q in order:
        here = lists[q] if own is None else tied(lists[q], own)
        there = to_copy(here)
        own = add_lists([here], own, None, half, capacity)
        copy = add_lists([there], copy, own if q == order[-1] else None, half, capacity)
    return update(copy, to_core(copy), weight, accum)


def solution(mesh):
    shards, reps = mesh.shape["shard"], mesh.shape["rep"]
    in_specs = (
        P(("shard", "rep"), None, None),
        P(("shard", "rep")),
        P(("shard", "rep"), None),
        P(("shard", "rep")),
        P("shard", None),
        P("shard"),
    )
    out_specs = (P("shard", None), P("shard"))
    paired = reps == 4 and shards == 8
    body = functools.partial(paired_body, shards, reps) if paired else general_body
    return jax.shard_map(body, mesh=mesh, in_specs=in_specs, out_specs=out_specs, check_vma=False)
```

```python
import functools

import jax
import jax.numpy as jnp
from jax import lax
from jax.experimental import pallas as pl
from jax.experimental.pallas import tpu as pltpu
from jax.sharding import PartitionSpec as P

step_size = 0.25
epsilon = 1e-08
f32, bf16, i32 = jnp.float32, jnp.bfloat16, jnp.int32
LANES = 128
PAD = 16
VMEM_LIMIT = 48 * 1024 * 1024
MEDIUM = pl.CostEstimate(flops=100_000_000, bytes_accessed=1024, transcendentals=0)
SMALL = pl.CostEstimate(flops=1024, bytes_accessed=1024, transcendentals=0)


def adagrad(weight, accum, table_grad):
    new_accum = accum + jnp.mean(table_grad * table_grad, axis=1)
    new_weight = weight - step_size * table_grad / (jnp.sqrt(new_accum)[:, None] + epsilon)
    return (new_weight, new_accum)


def general_body(grad_pooled, lookup_weight, owner, local_row, weight, accum):
    width = grad_pooled.shape[-1]
    lookups = lookup_weight.shape[0]
    pooling = lookups // (grad_pooled.shape[0] * grad_pooled.shape[1])
    shards = lax.axis_size("shard")
    capacity = (3 * lookups + 2 * shards - 1) // (2 * shards)
    bags = grad_pooled.reshape(-1, width).astype(f32)
    rows = (bags[:, None, :] * lookup_weight.reshape(-1, pooling, 1)).reshape(lookups, width)
    rows = rows.astype(bf16)
    target_shard = owner[:, 0]
    hits = (target_shard[:, None] == jnp.arange(shards, dtype=i32)[None, :]).astype(i32)
    ranks = jnp.sum(jnp.cumsum(hits, axis=0) * hits, axis=1) - 1
    slots = target_shard * capacity + ranks
    outgoing = jnp.zeros((shards * capacity, width), bf16).at[slots].set(rows)
    row_ids = jnp.full((shards * capacity,), -1, i32).at[slots].set(local_row)
    received, received_ids = (
        lax.all_to_all(outgoing.reshape(shards, capacity, width), "shard", split_axis=0, concat_axis=0, tiled=True),
        lax.all_to_all(row_ids.reshape(shards, capacity), "shard", split_axis=0, concat_axis=0, tiled=True),
    )
    flat_rows = received.reshape(-1, width)
    flat_ids = received_ids.reshape(-1)
    window_rows = weight.shape[0]
    span = 512
    starts = jnp.arange(window_rows // span, dtype=i32) * span

    def one_block(start):
        shifted = flat_ids - start
        onehot = (jnp.arange(span, dtype=i32)[:, None] == shifted[None, :]).astype(bf16)
        return jnp.dot(onehot, flat_rows, preferred_element_type=f32)

    partial_grad = lax.map(one_block, starts).reshape(window_rows, width)
    table_grad = lax.psum(partial_grad, "rep")
    return adagrad(weight, accum, table_grad)


def iota(shape, dim, dtype=i32):
    return lax.broadcasted_iota(i32, shape, dim).astype(dtype)


def pack_groups(groups, capacity, wanted, slot, ext_ref, out_ref):
    blocks = slot.shape[0]
    chunks = capacity // LANES
    place = iota((LANES, LANES), 0, f32)
    for n, g in enumerate(wanted):
        high, low = [], []
        for k in range(chunks):
            moved = slot - float(g * capacity + k * LANES)
            picks = jnp.concatenate(
                [(place == moved[r:r + 1, :]).astype(bf16) for r in range(blocks)], axis=1)
            packed = jnp.dot(picks, ext_ref[...], preferred_element_type=f32)
            out_ref[n, k * LANES:(k + 1) * LANES, :] = packed[:, :LANES].astype(bf16)
            turned = packed[:, LANES:].T
            high.append(turned[0:1])
            low.append(turned[1:2])
        out_ref[n, capacity:capacity + PAD, :] = jnp.concatenate(
            high + low + [jnp.zeros((PAD - 2 * chunks, LANES), f32)], axis=0).astype(bf16)


def rank_kernel(groups, capacity, code_ref, owner_ref, slot_ref):
    blocks = slot_ref.shape[0]
    wide = groups * blocks
    upper = (iota((LANES, LANES), 0) <= iota((LANES, LANES), 1)).astype(bf16)
    at, to = iota((wide, wide), 0), iota((wide, wide), 1)
    earlier = ((at // blocks == to // blocks) & (to < at)).astype(bf16)
    offset = owner_ref[...] ^ (code_ref[0] >> 1)
    group = jnp.where(offset < 2, offset, offset ^ (code_ref[0] & 1))
    hits = [(group == g).astype(f32) for g in range(groups)]
    stacked = jnp.concatenate(hits, axis=0).astype(bf16)
    inside = jnp.dot(stacked, upper, preferred_element_type=f32)
    totals = jnp.dot(stacked, jnp.ones((LANES, LANES), bf16), preferred_element_type=f32)
    carry = jnp.dot(earlier, totals.astype(bf16), preferred_element_type=f32)
    rank = inside + carry - 1.0
    slot = jnp.zeros((blocks, LANES), f32)
    for g in range(groups):
        slot = slot + hits[g] * (rank[g * blocks:(g + 1) * blocks] + float(g * capacity))
    slot_ref[...] = slot


def first_kernel(groups, capacity, wanted, slot_ref, row_ref, w_ref, bags_ref, out_ref, ext_ref):
    blocks = slot_ref.shape[0]
    lane = iota((LANES, LANES), 1)
    repeat = ((iota((LANES, LANES // 2), 0) >> 1) == iota((LANES, LANES // 2), 1)).astype(bf16)
    columns = jnp.concatenate(
        [(row_ref[...] >> 8).astype(f32), (row_ref[...] & 255).astype(f32), w_ref[...],
         jnp.zeros((LANES - 3 * blocks, LANES), f32)], axis=0).T
    for r in range(blocks):
        bag = jnp.dot(repeat, bags_ref[r * LANES // 2:(r + 1) * LANES // 2, :], preferred_element_type=f32)
        here = slice(r * LANES, (r + 1) * LANES)
        ext_ref[here, 0:LANES] = (bag * columns[:, 2 * blocks + r:2 * blocks + r + 1]).astype(bf16)
        high, low = columns[:, r:r + 1], columns[:, blocks + r:blocks + r + 1]
        ext_ref[here, LANES:2 * LANES] = jnp.where(
            lane == 0, high, jnp.where(lane == 1, low, 0.0)).astype(bf16)
    pack_groups(groups, capacity, wanted, slot_ref[...], ext_ref, out_ref)


def next_kernel(groups, capacity, wanted, slot_ref, ext_ref, *refs):
    out_ref = refs[-1]
    pack_groups(groups, capacity, wanted, slot_ref[...], ext_ref, out_ref)


def listed(wanted, capacity):
    return jax.ShapeDtypeStruct((len(wanted), capacity + PAD, LANES), bf16)


def find_slots(code, owner, groups, capacity):
    vmem = pl.BlockSpec(memory_space=pltpu.VMEM)
    return pl.pallas_call(
        functools.partial(rank_kernel, groups, capacity),
        out_shape=jax.ShapeDtypeStruct(owner.shape, f32),
        in_specs=[pl.BlockSpec(memory_space=pltpu.SMEM), vmem],
        out_specs=vmem,
        compiler_params=pltpu.CompilerParams(vmem_limit_bytes=VMEM_LIMIT),
        cost_estimate=pl.CostEstimate(flops=20_000_000_000, bytes_accessed=1024, transcendentals=0),
        name="find_slots",
    )(code, owner)


def pack_first(slot, local_row, lookup_weight, bags, groups, capacity, wanted):
    vmem = pl.BlockSpec(memory_space=pltpu.VMEM)
    return pl.pallas_call(
        functools.partial(first_kernel, groups, capacity, wanted),
        out_shape=[listed(wanted, capacity), jax.ShapeDtypeStruct((slot.size, 2 * LANES), bf16)],
        in_specs=[vmem] * 4,
        out_specs=[vmem, vmem],
        compiler_params=pltpu.CompilerParams(vmem_limit_bytes=VMEM_LIMIT),
        name="pack_first",
    )(slot, local_row, lookup_weight, bags)


def pack_next(slot, ext, groups, capacity, wanted, after=()):
    vmem = pl.BlockSpec(memory_space=pltpu.VMEM)
    return pl.pallas_call(
        functools.partial(next_kernel, groups, capacity, wanted),
        out_shape=listed(wanted, capacity),
        in_specs=[vmem, vmem] + [pl.BlockSpec(memory_space=pl.ANY)] * len(after),
        out_specs=vmem,
        compiler_params=pltpu.CompilerParams(vmem_limit_bytes=VMEM_LIMIT),
        cost_estimate=SMALL,
        name="pack_next",
    )(slot, ext, *after)


def add_kernel(capacity, lists, first, last, total, start, *refs):
    in_refs, refs = refs[:lists], list(refs[lists:])
    out_ref, rhs_ref = refs[-2:]
    before = None if first else refs.pop(0)
    beside = refs.pop(0) if last else None
    half = total
    chunks = capacity // LANES
    highs, lows = [], []
    at = 0
    for ref in in_refs:
        for part in range(ref.shape[0] // (capacity + PAD)):
            base = part * (capacity + PAD)
            digits = ref[base + capacity:base + capacity + PAD, :].astype(f32)
            high = digits[0:chunks]
            upper = (high >= float(half // 256)).astype(f32)
            high = high - upper * float(half // 256)
            highs += [high[k:k + 1] for k in range(chunks)]
            lows += [digits[chunks + k:chunks + k + 1] for k in range(chunks)]
            turned = jnp.concatenate([upper, jnp.zeros((LANES - chunks, LANES), f32)], axis=0).T
            for k in range(chunks):
                rows = ref[base + k * LANES:base + (k + 1) * LANES, :].astype(f32)
                above = turned[:, k:k + 1] > 0.5
                here = slice(at, at + LANES)
                rhs_ref[here, 0:LANES] = jnp.where(above, 0.0, rows).astype(bf16)
                rhs_ref[here, LANES:2 * LANES] = jnp.where(above, rows, 0.0).astype(bf16)
                at += LANES
    place = iota((256, LANES), 0, f32)
    for n in range(out_ref.shape[0] // 256):
        h = start + n
        picks = jnp.concatenate(
            [(place == jnp.where(hi == float(h), lo, -1.0)).astype(bf16) for hi, lo in zip(highs, lows)], axis=1)
        part = jnp.dot(picks, rhs_ref[...], preferred_element_type=f32)
        here = slice(h * 256, (h + 1) * 256)
        if before is not None:
            part = part + before[here, :]
        if beside is not None:
            part = part + beside[here, :]
        out_ref[n * 256:(n + 1) * 256, :] = part.astype(out_ref.dtype)


def add_lists(lists, before, beside, half, capacity, piece=0, pieces=1, after=()):
    vmem = pl.BlockSpec(memory_space=pltpu.VMEM)
    n = len(lists)
    depth = sum(value.shape[0] for value in lists) // (capacity + PAD) * capacity
    more = [value for value in (before, beside) if value is not None]
    return pl.pallas_call(
        functools.partial(add_kernel, capacity, n, before is None, beside is not None, half, piece * (half // pieces // 256)),
        out_shape=jax.ShapeDtypeStruct((half // pieces, 2 * LANES), f32 if beside is None else bf16),
        in_specs=[vmem] * (n + len(more)) + [pl.BlockSpec(memory_space=pl.ANY)] * len(after),
        out_specs=vmem,
        scratch_shapes=[pltpu.VMEM((depth, 2 * LANES), bf16)],
        input_output_aliases={n: 0} if beside is None and before is not None else {},
        compiler_params=pltpu.CompilerParams(vmem_limit_bytes=VMEM_LIMIT),
        cost_estimate=MEDIUM,
        name="add_lists",
    )(*lists, *more, *after)


def update_kernel(first, own_ref, other_ref, weight_ref, accum_ref, *refs):
    new_weight_hbm, new_accum_ref, out_ref, sems = refs[-4:]
    blocks = accum_ref.shape[0]
    span = own_ref.shape[0] // LANES
    lane = iota((LANES, LANES), 1)
    old = jnp.concatenate([accum_ref[...], jnp.zeros((LANES - blocks, LANES), f32)], axis=0).T
    new = old
    copies = []
    for side in range(2):
        base = side * (blocks // 2) + first * span

        def grad(n):
            at, to = slice(n * LANES, (n + 1) * LANES), slice(side * LANES, (side + 1) * LANES)
            return own_ref[at, to].astype(f32) + other_ref[at, to].astype(f32)

        for n in range(span):
            g = grad(n)
            new = jnp.where(lane == base + n, new + jnp.sum(g * g, axis=1, keepdims=True) * (1.0 / LANES), new)
        scale = step_size / (jnp.sqrt(new) + epsilon)
        for n in range(span):
            b = base + n
            out_ref[(side * span + n) * LANES:(side * span + n + 1) * LANES, :] = (
                weight_ref[b * LANES:(b + 1) * LANES, :] - grad(n) * scale[:, b:b + 1])
        copies.append(pltpu.make_async_copy(
            out_ref.at[side * span * LANES:(side + 1) * span * LANES],
            new_weight_hbm.at[base * LANES:(base + span) * LANES], sems.at[side]))
        copies[-1].start()
    new_accum_ref[...] = new.T[:blocks]
    for copy in copies:
        copy.wait()


def update(piece, own, other, weight, accum, so_far):
    vmem, hbm = pl.BlockSpec(memory_space=pltpu.VMEM), pl.BlockSpec(memory_space=pltpu.HBM)
    more = [] if so_far is None else [so_far]
    return pl.pallas_call(
        functools.partial(update_kernel, piece),
        out_shape=[jax.ShapeDtypeStruct(weight.shape, f32), jax.ShapeDtypeStruct(accum.shape, f32)],
        in_specs=[vmem] * 4 + [hbm] * len(more),
        out_specs=[hbm, vmem],
        scratch_shapes=[pltpu.VMEM((2 * own.shape[0], LANES), f32), pltpu.SemaphoreType.DMA((2,))],
        input_output_aliases={4: 0} if more else {},
        compiler_params=pltpu.CompilerParams(vmem_limit_bytes=VMEM_LIMIT),
        name="update",
    )(own, other, weight, accum, *more)


def tied(value, after):
    return value + (after[-1:, 0:LANES] * 0.0).astype(value.dtype)


def paired_body(shards, reps, grad_pooled, lookup_weight, owner, local_row, weight, accum):
    width = grad_pooled.shape[-1]
    lookups = lookup_weight.shape[0]
    capacity = (3 * lookups + 2 * shards - 1) // (2 * shards)
    half = weight.shape[0] // 2
    axes = ("shard", "rep")

    def permute(value, target):
        pairs = [(s * reps + r, target(s, r)) for s in range(shards) for r in range(reps)]
        return lax.ppermute(value, axes, pairs)

    to_core = functools.partial(permute, target=lambda s, r: s * reps + (r ^ 1))
    to_copy = functools.partial(permute, target=lambda s, r: s * reps + (r ^ 2))
    code = lax.axis_index("shard").astype(i32) * 2 + (lax.axis_index("rep").astype(i32) & 1)
    dense = (lookups // LANES, LANES)
    slot = find_slots(code.reshape(1), owner.reshape(dense), shards, capacity)

    def swapped(qs, pack_given, after):
        got = to_core(pack_given)
        keep = pack_next(slot, ext, shards, capacity, [2 * q for q in qs], after)
        return [jnp.concatenate([keep[n], got[n]], axis=0) for n in range(len(qs))]

    def send(q, payload):
        return permute(payload, lambda s, r: (s ^ (2 * q + (r & 1))) * reps + r)

    far = shards // 2 - 1
    near = [1, far - 1]
    given, ext = pack_first(slot, local_row.reshape(dense), lookup_weight.reshape(dense),
                            grad_pooled.reshape(-1, width), shards, capacity, [2 * far + 1])
    first = swapped([far], given, ())
    lists = {far: send(far, first[0])}
    given = pack_next(slot, ext, shards, capacity, [2 * q + 1 for q in near], first)
    got = to_core(given)
    kept = pack_next(slot, ext, shards, capacity, [2 * q for q in near], first)
    beside = pack_next(slot, ext, shards, capacity, [0, 1], [got])
    lists[0] = jnp.concatenate([beside[0], permute(beside[1], lambda s, r: (s ^ 1) * reps + r)], axis=0)
    for n, q in enumerate(near):
        lists[q] = send(q, jnp.concatenate([kept[n], got[n]], axis=0))

    last = far - 1
    there = to_copy(lists[0])
    own = add_lists([lists[0]], None, None, half, capacity)
    here_far = tied(lists[far], own)
    there_far = to_copy(here_far)
    here_near = tied(lists[1], here_far)
    there_near = to_copy(here_near)
    here_last = tied(lists[last], here_near)
    there_last = to_copy(here_last)
    own = add_lists([here_far, here_near], own, None, half, capacity, after=[here_last])
    copy = add_lists([there], None, None, half, capacity, after=[here_last])
    own = add_lists([here_last], own, None, half, capacity)
    copy = add_lists([there_far, there_near], copy, None, half, capacity)
    there = there_last

    pieces = 2
    sums = [add_lists([there], copy, own, half, capacity, n, pieces) for n in range(pieces)]
    others = [to_core(value) for value in sums]
    new_weight, new_accum = None, accum.reshape(-1, LANES)
    for n in range(pieces):
        new_weight, new_accum = update(n, sums[n], others[n], weight, new_accum, new_weight)
    return new_weight, new_accum.reshape(-1)


def solution(mesh):
    shards, reps = mesh.shape["shard"], mesh.shape["rep"]
    in_specs = (
        P(("shard", "rep"), None, None),
        P(("shard", "rep")),
        P(("shard", "rep"), None),
        P(("shard", "rep")),
        P("shard", None),
        P("shard"),
    )
    out_specs = (P("shard", None), P("shard"))
    paired = reps == 4 and shards == 8
    body = functools.partial(paired_body, shards, reps) if paired else general_body
    return jax.shard_map(body, mesh=mesh, in_specs=in_specs, out_specs=out_specs, check_vma=False)
```

```python
import functools

import jax
import jax.numpy as jnp
from jax import lax
from jax.experimental import pallas as pl
from jax.experimental.pallas import tpu as pltpu
from jax.sharding import PartitionSpec as P

step_size = 0.25
epsilon = 1e-08
f32, bf16, i32 = jnp.float32, jnp.bfloat16, jnp.int32
LANES = 128
PAD = 16
VMEM_LIMIT = 48 * 1024 * 1024
MEDIUM = pl.CostEstimate(flops=100_000_000, bytes_accessed=1024, transcendentals=0)
SMALL = pl.CostEstimate(flops=1024, bytes_accessed=1024, transcendentals=0)


def adagrad(weight, accum, table_grad):
    new_accum = accum + jnp.mean(table_grad * table_grad, axis=1)
    new_weight = weight - step_size * table_grad / (jnp.sqrt(new_accum)[:, None] + epsilon)
    return (new_weight, new_accum)


def general_body(grad_pooled, lookup_weight, owner, local_row, weight, accum):
    width = grad_pooled.shape[-1]
    lookups = lookup_weight.shape[0]
    pooling = lookups // (grad_pooled.shape[0] * grad_pooled.shape[1])
    shards = lax.axis_size("shard")
    capacity = (3 * lookups + 2 * shards - 1) // (2 * shards)
    bags = grad_pooled.reshape(-1, width).astype(f32)
    rows = (bags[:, None, :] * lookup_weight.reshape(-1, pooling, 1)).reshape(lookups, width)
    rows = rows.astype(bf16)
    target_shard = owner[:, 0]
    hits = (target_shard[:, None] == jnp.arange(shards, dtype=i32)[None, :]).astype(i32)
    ranks = jnp.sum(jnp.cumsum(hits, axis=0) * hits, axis=1) - 1
    slots = target_shard * capacity + ranks
    outgoing = jnp.zeros((shards * capacity, width), bf16).at[slots].set(rows)
    row_ids = jnp.full((shards * capacity,), -1, i32).at[slots].set(local_row)
    received, received_ids = (
        lax.all_to_all(outgoing.reshape(shards, capacity, width), "shard", split_axis=0, concat_axis=0, tiled=True),
        lax.all_to_all(row_ids.reshape(shards, capacity), "shard", split_axis=0, concat_axis=0, tiled=True),
    )
    flat_rows = received.reshape(-1, width)
    flat_ids = received_ids.reshape(-1)
    window_rows = weight.shape[0]
    span = 512
    starts = jnp.arange(window_rows // span, dtype=i32) * span

    def one_block(start):
        shifted = flat_ids - start
        onehot = (jnp.arange(span, dtype=i32)[:, None] == shifted[None, :]).astype(bf16)
        return jnp.dot(onehot, flat_rows, preferred_element_type=f32)

    partial_grad = lax.map(one_block, starts).reshape(window_rows, width)
    table_grad = lax.psum(partial_grad, "rep")
    return adagrad(weight, accum, table_grad)


def iota(shape, dim, dtype=i32):
    return lax.broadcasted_iota(i32, shape, dim).astype(dtype)


def pack_groups(groups, capacity, wanted, slot, ext_ref, out_ref):
    blocks = slot.shape[0]
    chunks = capacity // LANES
    place = iota((LANES, LANES), 0, f32)
    for n, g in enumerate(wanted):
        high, low = [], []
        for k in range(chunks):
            moved = slot - float(g * capacity + k * LANES)
            picks = jnp.concatenate(
                [(place == moved[r:r + 1, :]).astype(bf16) for r in range(blocks)], axis=1)
            packed = jnp.dot(picks, ext_ref[...], preferred_element_type=f32)
            out_ref[n, k * LANES:(k + 1) * LANES, :] = packed[:, :LANES].astype(bf16)
            turned = packed[:, LANES:].T
            high.append(turned[0:1])
            low.append(turned[1:2])
        out_ref[n, capacity:capacity + PAD, :] = jnp.concatenate(
            high + low + [jnp.zeros((PAD - 2 * chunks, LANES), f32)], axis=0).astype(bf16)


def rank_kernel(groups, capacity, code_ref, owner_ref, slot_ref):
    blocks = slot_ref.shape[0]
    wide = groups * blocks
    upper = (iota((LANES, LANES), 0) <= iota((LANES, LANES), 1)).astype(bf16)
    at, to = iota((wide, wide), 0), iota((wide, wide), 1)
    earlier = ((at // blocks == to // blocks) & (to < at)).astype(bf16)
    offset = owner_ref[...] ^ (code_ref[0] >> 1)
    group = jnp.where(offset < 2, offset, offset ^ (code_ref[0] & 1))
    hits = [(group == g).astype(f32) for g in range(groups)]
    stacked = jnp.concatenate(hits, axis=0).astype(bf16)
    inside = jnp.dot(stacked, upper, preferred_element_type=f32)
    totals = jnp.dot(stacked, jnp.ones((LANES, LANES), bf16), preferred_element_type=f32)
    carry = jnp.dot(earlier, totals.astype(bf16), preferred_element_type=f32)
    rank = inside + carry - 1.0
    slot = jnp.zeros((blocks, LANES), f32)
    for g in range(groups):
        slot = slot + hits[g] * (rank[g * blocks:(g + 1) * blocks] + float(g * capacity))
    slot_ref[...] = slot


def first_kernel(groups, capacity, wanted, slot_ref, row_ref, w_ref, bags_ref, out_ref, ext_ref):
    blocks = slot_ref.shape[0]
    lane = iota((LANES, LANES), 1)
    repeat = ((iota((LANES, LANES // 2), 0) >> 1) == iota((LANES, LANES // 2), 1)).astype(bf16)
    columns = jnp.concatenate(
        [(row_ref[...] >> 8).astype(f32), (row_ref[...] & 255).astype(f32), w_ref[...],
         jnp.zeros((LANES - 3 * blocks, LANES), f32)], axis=0).T
    for r in range(blocks):
        bag = jnp.dot(repeat, bags_ref[r * LANES // 2:(r + 1) * LANES // 2, :], preferred_element_type=f32)
        here = slice(r * LANES, (r + 1) * LANES)
        ext_ref[here, 0:LANES] = (bag * columns[:, 2 * blocks + r:2 * blocks + r + 1]).astype(bf16)
        high, low = columns[:, r:r + 1], columns[:, blocks + r:blocks + r + 1]
        ext_ref[here, LANES:2 * LANES] = jnp.where(
            lane == 0, high, jnp.where(lane == 1, low, 0.0)).astype(bf16)
    pack_groups(groups, capacity, wanted, slot_ref[...], ext_ref, out_ref)


def next_kernel(groups, capacity, wanted, slot_ref, ext_ref, *refs):
    out_ref = refs[-1]
    pack_groups(groups, capacity, wanted, slot_ref[...], ext_ref, out_ref)


def listed(wanted, capacity):
    return jax.ShapeDtypeStruct((len(wanted), capacity + PAD, LANES), bf16)


def find_slots(code, owner, groups, capacity):
    vmem = pl.BlockSpec(memory_space=pltpu.VMEM)
    return pl.pallas_call(
        functools.partial(rank_kernel, groups, capacity),
        out_shape=jax.ShapeDtypeStruct(owner.shape, f32),
        in_specs=[pl.BlockSpec(memory_space=pltpu.SMEM), vmem],
        out_specs=vmem,
        compiler_params=pltpu.CompilerParams(vmem_limit_bytes=VMEM_LIMIT),
        cost_estimate=pl.CostEstimate(flops=20_000_000_000, bytes_accessed=1024, transcendentals=0),
        name="find_slots",
    )(code, owner)


def pack_first(slot, local_row, lookup_weight, bags, groups, capacity, wanted):
    vmem = pl.BlockSpec(memory_space=pltpu.VMEM)
    return pl.pallas_call(
        functools.partial(first_kernel, groups, capacity, wanted),
        out_shape=[listed(wanted, capacity), jax.ShapeDtypeStruct((slot.size, 2 * LANES), bf16)],
        in_specs=[vmem] * 4,
        out_specs=[vmem, vmem],
        compiler_params=pltpu.CompilerParams(vmem_limit_bytes=VMEM_LIMIT),
        name="pack_first",
    )(slot, local_row, lookup_weight, bags)


def pack_next(slot, ext, groups, capacity, wanted, after=()):
    vmem = pl.BlockSpec(memory_space=pltpu.VMEM)
    return pl.pallas_call(
        functools.partial(next_kernel, groups, capacity, wanted),
        out_shape=listed(wanted, capacity),
        in_specs=[vmem, vmem] + [pl.BlockSpec(memory_space=pl.ANY)] * len(after),
        out_specs=vmem,
        compiler_params=pltpu.CompilerParams(vmem_limit_bytes=VMEM_LIMIT),
        cost_estimate=SMALL,
        name="pack_next",
    )(slot, ext, *after)


def add_kernel(capacity, lists, first, last, total, start, *refs):
    in_refs, refs = refs[:lists], list(refs[lists:])
    out_ref, rhs_ref = refs[-2:]
    before = None if first else refs.pop(0)
    beside = refs.pop(0) if last else None
    half = total
    chunks = capacity // LANES
    highs, lows = [], []
    at = 0
    for ref in in_refs:
        for part in range(ref.shape[0] // (capacity + PAD)):
            base = part * (capacity + PAD)
            digits = ref[base + capacity:base + capacity + PAD, :].astype(f32)
            high = digits[0:chunks]
            upper = (high >= float(half // 256)).astype(f32)
            high = high - upper * float(half // 256)
            highs += [high[k:k + 1] for k in range(chunks)]
            lows += [digits[chunks + k:chunks + k + 1] for k in range(chunks)]
            turned = jnp.concatenate([upper, jnp.zeros((LANES - chunks, LANES), f32)], axis=0).T
            for k in range(chunks):
                rows = ref[base + k * LANES:base + (k + 1) * LANES, :].astype(f32)
                above = turned[:, k:k + 1] > 0.5
                here = slice(at, at + LANES)
                rhs_ref[here, 0:LANES] = jnp.where(above, 0.0, rows).astype(bf16)
                rhs_ref[here, LANES:2 * LANES] = jnp.where(above, rows, 0.0).astype(bf16)
                at += LANES
    place = iota((256, LANES), 0, f32)
    for n in range(out_ref.shape[0] // 256):
        h = start + n
        picks = jnp.concatenate(
            [(place == jnp.where(hi == float(h), lo, -1.0)).astype(bf16) for hi, lo in zip(highs, lows)], axis=1)
        part = jnp.dot(picks, rhs_ref[...], preferred_element_type=f32)
        here = slice(h * 256, (h + 1) * 256)
        if before is not None:
            part = part + before[here, :]
        if beside is not None:
            part = part + beside[here, :]
        out_ref[n * 256:(n + 1) * 256, :] = part.astype(out_ref.dtype)


def add_lists(lists, before, beside, half, capacity, piece=0, pieces=1, after=()):
    vmem = pl.BlockSpec(memory_space=pltpu.VMEM)
    n = len(lists)
    depth = sum(value.shape[0] for value in lists) // (capacity + PAD) * capacity
    more = [value for value in (before, beside) if value is not None]
    return pl.pallas_call(
        functools.partial(add_kernel, capacity, n, before is None, beside is not None, half, piece * (half // pieces // 256)),
        out_shape=jax.ShapeDtypeStruct((half // pieces, 2 * LANES), f32 if beside is None else bf16),
        in_specs=[vmem] * (n + len(more)) + [pl.BlockSpec(memory_space=pl.ANY)] * len(after),
        out_specs=vmem,
        scratch_shapes=[pltpu.VMEM((depth, 2 * LANES), bf16)],
        input_output_aliases={n: 0} if beside is None and before is not None else {},
        compiler_params=pltpu.CompilerParams(vmem_limit_bytes=VMEM_LIMIT),
        cost_estimate=MEDIUM,
        name="add_lists",
    )(*lists, *more, *after)


def update_kernel(first, own_ref, other_ref, weight_ref, accum_ref, *refs):
    new_weight_hbm, new_accum_ref, out_ref, sems = refs[-4:]
    blocks = accum_ref.shape[0]
    span = own_ref.shape[0] // LANES
    lane = iota((LANES, LANES), 1)
    old = jnp.concatenate([accum_ref[...], jnp.zeros((LANES - blocks, LANES), f32)], axis=0).T
    new = old
    copies = []
    for side in range(2):
        base = side * (blocks // 2) + first * span

        def grad(n):
            at, to = slice(n * LANES, (n + 1) * LANES), slice(side * LANES, (side + 1) * LANES)
            return own_ref[at, to].astype(f32) + other_ref[at, to].astype(f32)

        for n in range(span):
            g = grad(n)
            new = jnp.where(lane == base + n, new + jnp.sum(g * g, axis=1, keepdims=True) * (1.0 / LANES), new)
        scale = step_size / (jnp.sqrt(new) + epsilon)
        for n in range(span):
            b = base + n
            out_ref[(side * span + n) * LANES:(side * span + n + 1) * LANES, :] = (
                weight_ref[b * LANES:(b + 1) * LANES, :] - grad(n) * scale[:, b:b + 1])
        copies.append(pltpu.make_async_copy(
            out_ref.at[side * span * LANES:(side + 1) * span * LANES],
            new_weight_hbm.at[base * LANES:(base + span) * LANES], sems.at[side]))
        copies[-1].start()
    new_accum_ref[...] = new.T[:blocks]
    for copy in copies:
        copy.wait()


def update(piece, own, other, weight, accum, so_far):
    vmem, hbm = pl.BlockSpec(memory_space=pltpu.VMEM), pl.BlockSpec(memory_space=pltpu.HBM)
    more = [] if so_far is None else [so_far]
    return pl.pallas_call(
        functools.partial(update_kernel, piece),
        out_shape=[jax.ShapeDtypeStruct(weight.shape, f32), jax.ShapeDtypeStruct(accum.shape, f32)],
        in_specs=[vmem] * 4 + [hbm] * len(more),
        out_specs=[hbm, vmem],
        scratch_shapes=[pltpu.VMEM((2 * own.shape[0], LANES), f32), pltpu.SemaphoreType.DMA((2,))],
        input_output_aliases={4: 0} if more else {},
        compiler_params=pltpu.CompilerParams(vmem_limit_bytes=VMEM_LIMIT),
        name="update",
    )(own, other, weight, accum, *more)


def tied(value, after):
    return value + (after[-1:, 0:LANES] * 0.0).astype(value.dtype)


def paired_body(shards, reps, grad_pooled, lookup_weight, owner, local_row, weight, accum):
    width = grad_pooled.shape[-1]
    lookups = lookup_weight.shape[0]
    capacity = (3 * lookups + 2 * shards - 1) // (2 * shards)
    half = weight.shape[0] // 2
    axes = ("shard", "rep")

    def permute(value, target):
        pairs = [(s * reps + r, target(s, r)) for s in range(shards) for r in range(reps)]
        return lax.ppermute(value, axes, pairs)

    to_core = functools.partial(permute, target=lambda s, r: s * reps + (r ^ 1))
    to_copy = functools.partial(permute, target=lambda s, r: s * reps + (r ^ 2))
    code = lax.axis_index("shard").astype(i32) * 2 + (lax.axis_index("rep").astype(i32) & 1)
    dense = (lookups // LANES, LANES)
    slot = find_slots(code.reshape(1), owner.reshape(dense), shards, capacity)

    def swapped(qs, pack_given, after):
        got = to_core(pack_given)
        keep = pack_next(slot, ext, shards, capacity, [2 * q for q in qs], after)
        return [jnp.concatenate([keep[n], got[n]], axis=0) for n in range(len(qs))]

    def send(q, payload):
        return permute(payload, lambda s, r: (s ^ (2 * q + (r & 1))) * reps + r)

    far = shards // 2 - 1
    near = [1, far - 1]
    given, ext = pack_first(slot, local_row.reshape(dense), lookup_weight.reshape(dense),
                            grad_pooled.reshape(-1, width), shards, capacity, [2 * far + 1])
    first = swapped([far], given, ())
    lists = {far: send(far, first[0])}
    given = pack_next(slot, ext, shards, capacity, [2 * q + 1 for q in near], first)
    got = to_core(given)
    kept = pack_next(slot, ext, shards, capacity, [2 * q for q in near], first)
    beside = pack_next(slot, ext, shards, capacity, [0, 1], [got])
    lists[0] = jnp.concatenate([beside[0], permute(beside[1], lambda s, r: (s ^ 1) * reps + r)], axis=0)
    for n, q in enumerate(near):
        lists[q] = send(q, jnp.concatenate([kept[n], got[n]], axis=0))

    last = far - 1
    there = to_copy(lists[0])
    own = add_lists([lists[0]], None, None, half, capacity)
    here_far = tied(lists[far], own)
    there_far = to_copy(here_far)
    here_near = tied(lists[1], here_far)
    there_near = to_copy(here_near)
    own = add_lists([here_far], own, None, half, capacity, after=[here_near])
    copy = add_lists([there], None, None, half, capacity, after=[here_near])
    here_last = tied(lists[last], own)
    there_last = to_copy(here_last)
    own = add_lists([here_near], own, None, half, capacity, after=[here_last])
    copy = add_lists([there_far], copy, None, half, capacity, after=[here_last])
    own = add_lists([here_last], own, None, half, capacity)
    copy = add_lists([there_near], copy, None, half, capacity)
    there = there_last

    pieces = 2
    sums = [add_lists([there], copy, own, half, capacity, n, pieces) for n in range(pieces)]
    others = [to_core(value) for value in sums]
    new_weight, new_accum = None, accum.reshape(-1, LANES)
    for n in range(pieces):
        new_weight, new_accum = update(n, sums[n], others[n], weight, new_accum, new_weight)
    return new_weight, new_accum.reshape(-1)


def solution(mesh):
    shards, reps = mesh.shape["shard"], mesh.shape["rep"]
    in_specs = (
        P(("shard", "rep"), None, None),
        P(("shard", "rep")),
        P(("shard", "rep"), None),
        P(("shard", "rep")),
        P("shard", None),
        P("shard"),
    )
    out_specs = (P("shard", None), P("shard"))
    paired = reps == 4 and shards == 8
    body = functools.partial(paired_body, shards, reps) if paired else general_body
    return jax.shard_map(body, mesh=mesh, in_specs=in_specs, out_specs=out_specs, check_vma=False)
```

```python
import functools

import jax
import jax.numpy as jnp
from jax import lax
from jax.experimental import pallas as pl
from jax.experimental.pallas import tpu as pltpu
from jax.sharding import PartitionSpec as P

step_size = 0.25
epsilon = 1e-08
f32, bf16, i32 = jnp.float32, jnp.bfloat16, jnp.int32
LANES = 128
PAD = 16
VMEM_LIMIT = 48 * 1024 * 1024
MEDIUM = pl.CostEstimate(flops=100_000_000, bytes_accessed=1024, transcendentals=0)
SMALL = pl.CostEstimate(flops=1024, bytes_accessed=1024, transcendentals=0)


def adagrad(weight, accum, table_grad):
    new_accum = accum + jnp.mean(table_grad * table_grad, axis=1)
    new_weight = weight - step_size * table_grad / (jnp.sqrt(new_accum)[:, None] + epsilon)
    return (new_weight, new_accum)


def general_body(grad_pooled, lookup_weight, owner, local_row, weight, accum):
    width = grad_pooled.shape[-1]
    lookups = lookup_weight.shape[0]
    pooling = lookups // (grad_pooled.shape[0] * grad_pooled.shape[1])
    shards = lax.axis_size("shard")
    capacity = (3 * lookups + 2 * shards - 1) // (2 * shards)
    bags = grad_pooled.reshape(-1, width).astype(f32)
    rows = (bags[:, None, :] * lookup_weight.reshape(-1, pooling, 1)).reshape(lookups, width)
    rows = rows.astype(bf16)
    target_shard = owner[:, 0]
    hits = (target_shard[:, None] == jnp.arange(shards, dtype=i32)[None, :]).astype(i32)
    ranks = jnp.sum(jnp.cumsum(hits, axis=0) * hits, axis=1) - 1
    slots = target_shard * capacity + ranks
    outgoing = jnp.zeros((shards * capacity, width), bf16).at[slots].set(rows)
    row_ids = jnp.full((shards * capacity,), -1, i32).at[slots].set(local_row)
    received, received_ids = (
        lax.all_to_all(outgoing.reshape(shards, capacity, width), "shard", split_axis=0, concat_axis=0, tiled=True),
        lax.all_to_all(row_ids.reshape(shards, capacity), "shard", split_axis=0, concat_axis=0, tiled=True),
    )
    flat_rows = received.reshape(-1, width)
    flat_ids = received_ids.reshape(-1)
    window_rows = weight.shape[0]
    span = 512
    starts = jnp.arange(window_rows // span, dtype=i32) * span

    def one_block(start):
        shifted = flat_ids - start
        onehot = (jnp.arange(span, dtype=i32)[:, None] == shifted[None, :]).astype(bf16)
        return jnp.dot(onehot, flat_rows, preferred_element_type=f32)

    partial_grad = lax.map(one_block, starts).reshape(window_rows, width)
    table_grad = lax.psum(partial_grad, "rep")
    return adagrad(weight, accum, table_grad)


def iota(shape, dim, dtype=i32):
    return lax.broadcasted_iota(i32, shape, dim).astype(dtype)


def pack_groups(groups, capacity, wanted, slot, ext_ref, out_ref):
    blocks = slot.shape[0]
    chunks = capacity // LANES
    place = iota((LANES, LANES), 0, f32)
    for n, g in enumerate(wanted):
        high, low = [], []
        for k in range(chunks):
            moved = slot - float(g * capacity + k * LANES)
            picks = jnp.concatenate(
                [(place == moved[r:r + 1, :]).astype(bf16) for r in range(blocks)], axis=1)
            packed = jnp.dot(picks, ext_ref[...], preferred_element_type=f32)
            out_ref[n, k * LANES:(k + 1) * LANES, :] = packed[:, :LANES].astype(bf16)
            turned = packed[:, LANES:].T
            high.append(turned[0:1])
            low.append(turned[1:2])
        out_ref[n, capacity:capacity + PAD, :] = jnp.concatenate(
            high + low + [jnp.zeros((PAD - 2 * chunks, LANES), f32)], axis=0).astype(bf16)


def rank_kernel(groups, capacity, code_ref, owner_ref, slot_ref):
    blocks = slot_ref.shape[0]
    wide = groups * blocks
    upper = (iota((LANES, LANES), 0) <= iota((LANES, LANES), 1)).astype(bf16)
    at, to = iota((wide, wide), 0), iota((wide, wide), 1)
    earlier = ((at // blocks == to // blocks) & (to < at)).astype(bf16)
    offset = owner_ref[...] ^ (code_ref[0] >> 1)
    group = jnp.where(offset < 2, offset, offset ^ (code_ref[0] & 1))
    hits = [(group == g).astype(f32) for g in range(groups)]
    stacked = jnp.concatenate(hits, axis=0).astype(bf16)
    inside = jnp.dot(stacked, upper, preferred_element_type=f32)
    totals = jnp.dot(stacked, jnp.ones((LANES, LANES), bf16), preferred_element_type=f32)
    carry = jnp.dot(earlier, totals.astype(bf16), preferred_element_type=f32)
    rank = inside + carry - 1.0
    slot = jnp.zeros((blocks, LANES), f32)
    for g in range(groups):
        slot = slot + hits[g] * (rank[g * blocks:(g + 1) * blocks] + float(g * capacity))
    slot_ref[...] = slot


def first_kernel(groups, capacity, wanted, slot_ref, row_ref, w_ref, bags_ref, out_ref, ext_ref):
    blocks = slot_ref.shape[0]
    lane = iota((LANES, LANES), 1)
    repeat = ((iota((LANES, LANES // 2), 0) >> 1) == iota((LANES, LANES // 2), 1)).astype(bf16)
    columns = jnp.concatenate(
        [(row_ref[...] >> 8).astype(f32), (row_ref[...] & 255).astype(f32), w_ref[...],
         jnp.zeros((LANES - 3 * blocks, LANES), f32)], axis=0).T
    for r in range(blocks):
        bag = jnp.dot(repeat, bags_ref[r * LANES // 2:(r + 1) * LANES // 2, :], preferred_element_type=f32)
        here = slice(r * LANES, (r + 1) * LANES)
        ext_ref[here, 0:LANES] = (bag * columns[:, 2 * blocks + r:2 * blocks + r + 1]).astype(bf16)
        high, low = columns[:, r:r + 1], columns[:, blocks + r:blocks + r + 1]
        ext_ref[here, LANES:2 * LANES] = jnp.where(
            lane == 0, high, jnp.where(lane == 1, low, 0.0)).astype(bf16)
    pack_groups(groups, capacity, wanted, slot_ref[...], ext_ref, out_ref)


def next_kernel(groups, capacity, wanted, slot_ref, ext_ref, *refs):
    out_ref = refs[-1]
    pack_groups(groups, capacity, wanted, slot_ref[...], ext_ref, out_ref)


def listed(wanted, capacity):
    return jax.ShapeDtypeStruct((len(wanted), capacity + PAD, LANES), bf16)


def find_slots(code, owner, groups, capacity):
    vmem = pl.BlockSpec(memory_space=pltpu.VMEM)
    return pl.pallas_call(
        functools.partial(rank_kernel, groups, capacity),
        out_shape=jax.ShapeDtypeStruct(owner.shape, f32),
        in_specs=[pl.BlockSpec(memory_space=pltpu.SMEM), vmem],
        out_specs=vmem,
        compiler_params=pltpu.CompilerParams(vmem_limit_bytes=VMEM_LIMIT),
        cost_estimate=pl.CostEstimate(flops=20_000_000_000, bytes_accessed=1024, transcendentals=0),
        name="find_slots",
    )(code, owner)


def pack_first(slot, local_row, lookup_weight, bags, groups, capacity, wanted):
    vmem = pl.BlockSpec(memory_space=pltpu.VMEM)
    return pl.pallas_call(
        functools.partial(first_kernel, groups, capacity, wanted),
        out_shape=[listed(wanted, capacity), jax.ShapeDtypeStruct((slot.size, 2 * LANES), bf16)],
        in_specs=[vmem] * 4,
        out_specs=[vmem, vmem],
        compiler_params=pltpu.CompilerParams(vmem_limit_bytes=VMEM_LIMIT),
        name="pack_first",
    )(slot, local_row, lookup_weight, bags)


def pack_next(slot, ext, groups, capacity, wanted, after=()):
    vmem = pl.BlockSpec(memory_space=pltpu.VMEM)
    return pl.pallas_call(
        functools.partial(next_kernel, groups, capacity, wanted),
        out_shape=listed(wanted, capacity),
        in_specs=[vmem, vmem] + [pl.BlockSpec(memory_space=pl.ANY)] * len(after),
        out_specs=vmem,
        compiler_params=pltpu.CompilerParams(vmem_limit_bytes=VMEM_LIMIT),
        cost_estimate=SMALL,
        name="pack_next",
    )(slot, ext, *after)


def add_kernel(capacity, lists, first, last, total, start, *refs):
    in_refs, refs = refs[:lists], list(refs[lists:])
    out_ref, rhs_ref = refs[-2:]
    before = None if first else refs.pop(0)
    beside = refs.pop(0) if last else None
    half = total
    chunks = capacity // LANES
    highs, lows = [], []
    at = 0
    for ref in in_refs:
        for part in range(ref.shape[0] // (capacity + PAD)):
            base = part * (capacity + PAD)
            digits = ref[base + capacity:base + capacity + PAD, :].astype(f32)
            high = digits[0:chunks]
            upper = (high >= float(half // 256)).astype(f32)
            high = high - upper * float(half // 256)
            highs += [high[k:k + 1] for k in range(chunks)]
            lows += [digits[chunks + k:chunks + k + 1] for k in range(chunks)]
            turned = jnp.concatenate([upper, jnp.zeros((LANES - chunks, LANES), f32)], axis=0).T
            for k in range(chunks):
                rows = ref[base + k * LANES:base + (k + 1) * LANES, :].astype(f32)
                above = turned[:, k:k + 1] > 0.5
                here = slice(at, at + LANES)
                rhs_ref[here, 0:LANES] = jnp.where(above, 0.0, rows).astype(bf16)
                rhs_ref[here, LANES:2 * LANES] = jnp.where(above, rows, 0.0).astype(bf16)
                at += LANES
    place = iota((256, LANES), 0, f32)
    for n in range(out_ref.shape[0] // 256):
        h = start + n
        picks = jnp.concatenate(
            [(place == jnp.where(hi == float(h), lo, -1.0)).astype(bf16) for hi, lo in zip(highs, lows)], axis=1)
        part = jnp.dot(picks, rhs_ref[...], preferred_element_type=f32)
        here = slice(h * 256, (h + 1) * 256)
        if before is not None:
            part = part + before[here, :]
        if beside is not None:
            part = part + beside[here, :]
        out_ref[n * 256:(n + 1) * 256, :] = part.astype(out_ref.dtype)


def add_lists(lists, before, beside, half, capacity, piece=0, pieces=1, after=()):
    vmem = pl.BlockSpec(memory_space=pltpu.VMEM)
    n = len(lists)
    depth = sum(value.shape[0] for value in lists) // (capacity + PAD) * capacity
    more = [value for value in (before, beside) if value is not None]
    return pl.pallas_call(
        functools.partial(add_kernel, capacity, n, before is None, beside is not None, half, piece * (half // pieces // 256)),
        out_shape=jax.ShapeDtypeStruct((half // pieces, 2 * LANES), f32 if beside is None else bf16),
        in_specs=[vmem] * (n + len(more)) + [pl.BlockSpec(memory_space=pl.ANY)] * len(after),
        out_specs=vmem,
        scratch_shapes=[pltpu.VMEM((depth, 2 * LANES), bf16)],
        input_output_aliases={n: 0} if beside is None and before is not None else {},
        compiler_params=pltpu.CompilerParams(vmem_limit_bytes=VMEM_LIMIT),
        cost_estimate=MEDIUM,
        name="add_lists",
    )(*lists, *more, *after)


def update_kernel(first, own_ref, other_ref, weight_ref, accum_ref, *refs):
    new_weight_hbm, new_accum_hbm, out_ref, new_accum_ref, sems = refs[-5:]
    blocks = accum_ref.shape[0]
    span = own_ref.shape[0] // LANES
    lane = iota((LANES, LANES), 1)
    old = jnp.concatenate([accum_ref[...], jnp.zeros((LANES - blocks, LANES), f32)], axis=0).T
    new = old
    copies = []
    for side in range(2):
        base = side * (blocks // 2) + first * span

        def grad(n):
            at, to = slice(n * LANES, (n + 1) * LANES), slice(side * LANES, (side + 1) * LANES)
            return own_ref[at, to].astype(f32) + other_ref[at, to].astype(f32)

        for n in range(span):
            g = grad(n)
            new = jnp.where(lane == base + n, new + jnp.sum(g * g, axis=1, keepdims=True) * (1.0 / LANES), new)
        scale = step_size / (jnp.sqrt(new) + epsilon)
        for n in range(span):
            b = base + n
            out_ref[(side * span + n) * LANES:(side * span + n + 1) * LANES, :] = (
                weight_ref[b * LANES:(b + 1) * LANES, :] - grad(n) * scale[:, b:b + 1])
        copies.append(pltpu.make_async_copy(
            out_ref.at[side * span * LANES:(side + 1) * span * LANES],
            new_weight_hbm.at[base * LANES:(base + span) * LANES], sems.at[side]))
        copies[-1].start()
    new_accum_ref[...] = new.T[:blocks]
    copies.append(pltpu.make_async_copy(new_accum_ref, new_accum_hbm, sems.at[2]))
    copies[-1].start()
    for copy in copies:
        copy.wait()


def update(piece, own, other, weight, accum, so_far):
    vmem, hbm = pl.BlockSpec(memory_space=pltpu.VMEM), pl.BlockSpec(memory_space=pltpu.HBM)
    more = [] if so_far is None else [so_far]
    return pl.pallas_call(
        functools.partial(update_kernel, piece),
        out_shape=[jax.ShapeDtypeStruct(weight.shape, f32), jax.ShapeDtypeStruct(accum.shape, f32)],
        in_specs=[vmem] * 4 + [hbm] * len(more),
        out_specs=[hbm, pl.BlockSpec(memory_space=pl.ANY)],
        scratch_shapes=[pltpu.VMEM((2 * own.shape[0], LANES), f32), pltpu.VMEM(accum.shape, f32),
                        pltpu.SemaphoreType.DMA((3,))],
        input_output_aliases={4: 0} if more else {},
        compiler_params=pltpu.CompilerParams(vmem_limit_bytes=VMEM_LIMIT),
        name="update",
    )(own, other, weight, accum, *more)


def tied(value, after):
    return value + (after[-1:, 0:LANES] * 0.0).astype(value.dtype)


def paired_body(shards, reps, grad_pooled, lookup_weight, owner, local_row, weight, accum):
    width = grad_pooled.shape[-1]
    lookups = lookup_weight.shape[0]
    capacity = (3 * lookups + 2 * shards - 1) // (2 * shards)
    half = weight.shape[0] // 2
    axes = ("shard", "rep")

    def permute(value, target):
        pairs = [(s * reps + r, target(s, r)) for s in range(shards) for r in range(reps)]
        return lax.ppermute(value, axes, pairs)

    to_core = functools.partial(permute, target=lambda s, r: s * reps + (r ^ 1))
    to_copy = functools.partial(permute, target=lambda s, r: s * reps + (r ^ 2))
    code = lax.axis_index("shard").astype(i32) * 2 + (lax.axis_index("rep").astype(i32) & 1)
    dense = (lookups // LANES, LANES)
    slot = find_slots(code.reshape(1), owner.reshape(dense), shards, capacity)

    def swapped(qs, pack_given, after):
        got = to_core(pack_given)
        keep = pack_next(slot, ext, shards, capacity, [2 * q for q in qs], after)
        return [jnp.concatenate([keep[n], got[n]], axis=0) for n in range(len(qs))]

    def send(q, payload):
        return permute(payload, lambda s, r: (s ^ (2 * q + (r & 1))) * reps + r)

    far = shards // 2 - 1
    near = [1, far - 1]
    given, ext = pack_first(slot, local_row.reshape(dense), lookup_weight.reshape(dense),
                            grad_pooled.reshape(-1, width), shards, capacity, [2 * far + 1])
    first = swapped([far], given, ())
    lists = {far: send(far, first[0])}
    given = pack_next(slot, ext, shards, capacity, [2 * q + 1 for q in near], first)
    got = to_core(given)
    kept = pack_next(slot, ext, shards, capacity, [2 * q for q in near], first)
    beside = pack_next(slot, ext, shards, capacity, [0, 1], [got])
    lists[0] = jnp.concatenate([beside[0], permute(beside[1], lambda s, r: (s ^ 1) * reps + r)], axis=0)
    for n, q in enumerate(near):
        lists[q] = send(q, jnp.concatenate([kept[n], got[n]], axis=0))

    last = far - 1
    there = to_copy(lists[0])
    own = add_lists([lists[0]], None, None, half, capacity)
    here_far = tied(lists[far], own)
    there_far = to_copy(here_far)
    here_near = tied(lists[1], here_far)
    there_near = to_copy(here_near)
    own = add_lists([here_far], own, None, half, capacity, after=[here_near])
    copy = add_lists([there], None, None, half, capacity, after=[here_near])
    here_last = tied(lists[last], own)
    there_last = to_copy(here_last)
    own = add_lists([here_near], own, None, half, capacity, after=[here_last])
    copy = add_lists([there_far], copy, None, half, capacity, after=[here_last])
    own = add_lists([here_last], own, None, half, capacity)
    copy = add_lists([there_near], copy, None, half, capacity)
    there = there_last

    pieces = 2
    sums = [add_lists([there], copy, own, half, capacity, n, pieces) for n in range(pieces)]
    others = [to_core(value) for value in sums]
    new_weight, new_accum = None, accum.reshape(-1, LANES)
    for n in range(pieces):
        new_weight, new_accum = update(n, sums[n], others[n], weight, new_accum, new_weight)
    return new_weight, new_accum.reshape(-1)


def solution(mesh):
    shards, reps = mesh.shape["shard"], mesh.shape["rep"]
    in_specs = (
        P(("shard", "rep"), None, None),
        P(("shard", "rep")),
        P(("shard", "rep"), None),
        P(("shard", "rep")),
        P("shard", None),
        P("shard"),
    )
    out_specs = (P("shard", None), P("shard"))
    paired = reps == 4 and shards == 8
    body = functools.partial(paired_body, shards, reps) if paired else general_body
    return jax.shard_map(body, mesh=mesh, in_specs=in_specs, out_specs=out_specs, check_vma=False)
```

```python
import functools

import jax
import jax.numpy as jnp
from jax import lax
from jax.experimental import pallas as pl
from jax.experimental.pallas import tpu as pltpu
from jax.sharding import PartitionSpec as P

step_size = 0.25
epsilon = 1e-08
f32, bf16, i32 = jnp.float32, jnp.bfloat16, jnp.int32
LANES = 128
PAD = 16
VMEM_LIMIT = 48 * 1024 * 1024
MEDIUM = pl.CostEstimate(flops=100_000_000, bytes_accessed=1024, transcendentals=0)
SMALL = pl.CostEstimate(flops=1024, bytes_accessed=1024, transcendentals=0)


def adagrad(weight, accum, table_grad):
    new_accum = accum + jnp.mean(table_grad * table_grad, axis=1)
    new_weight = weight - step_size * table_grad / (jnp.sqrt(new_accum)[:, None] + epsilon)
    return (new_weight, new_accum)


def general_body(grad_pooled, lookup_weight, owner, local_row, weight, accum):
    width = grad_pooled.shape[-1]
    lookups = lookup_weight.shape[0]
    pooling = lookups // (grad_pooled.shape[0] * grad_pooled.shape[1])
    shards = lax.axis_size("shard")
    capacity = (3 * lookups + 2 * shards - 1) // (2 * shards)
    bags = grad_pooled.reshape(-1, width).astype(f32)
    rows = (bags[:, None, :] * lookup_weight.reshape(-1, pooling, 1)).reshape(lookups, width)
    rows = rows.astype(bf16)
    target_shard = owner[:, 0]
    hits = (target_shard[:, None] == jnp.arange(shards, dtype=i32)[None, :]).astype(i32)
    ranks = jnp.sum(jnp.cumsum(hits, axis=0) * hits, axis=1) - 1
    slots = target_shard * capacity + ranks
    outgoing = jnp.zeros((shards * capacity, width), bf16).at[slots].set(rows)
    row_ids = jnp.full((shards * capacity,), -1, i32).at[slots].set(local_row)
    received, received_ids = (
        lax.all_to_all(outgoing.reshape(shards, capacity, width), "shard", split_axis=0, concat_axis=0, tiled=True),
        lax.all_to_all(row_ids.reshape(shards, capacity), "shard", split_axis=0, concat_axis=0, tiled=True),
    )
    flat_rows = received.reshape(-1, width)
    flat_ids = received_ids.reshape(-1)
    window_rows = weight.shape[0]
    span = 512
    starts = jnp.arange(window_rows // span, dtype=i32) * span

    def one_block(start):
        shifted = flat_ids - start
        onehot = (jnp.arange(span, dtype=i32)[:, None] == shifted[None, :]).astype(bf16)
        return jnp.dot(onehot, flat_rows, preferred_element_type=f32)

    partial_grad = lax.map(one_block, starts).reshape(window_rows, width)
    table_grad = lax.psum(partial_grad, "rep")
    return adagrad(weight, accum, table_grad)


def iota(shape, dim, dtype=i32):
    return lax.broadcasted_iota(i32, shape, dim).astype(dtype)


def pack_groups(groups, capacity, wanted, slot, ext_ref, out_ref):
    blocks = slot.shape[0]
    chunks = capacity // LANES
    place = iota((LANES, LANES), 0, f32)
    for n, g in enumerate(wanted):
        high, low = [], []
        for k in range(chunks):
            moved = slot - float(g * capacity + k * LANES)
            picks = jnp.concatenate(
                [(place == moved[r:r + 1, :]).astype(bf16) for r in range(blocks)], axis=1)
            packed = jnp.dot(picks, ext_ref[...], preferred_element_type=f32)
            out_ref[n, k * LANES:(k + 1) * LANES, :] = packed[:, :LANES].astype(bf16)
            turned = packed[:, LANES:].T
            high.append(turned[0:1])
            low.append(turned[1:2])
        out_ref[n, capacity:capacity + PAD, :] = jnp.concatenate(
            high + low + [jnp.zeros((PAD - 2 * chunks, LANES), f32)], axis=0).astype(bf16)


def rank_kernel(groups, capacity, code_ref, owner_ref, slot_ref):
    blocks = slot_ref.shape[0]
    wide = groups * blocks
    upper = (iota((LANES, LANES), 0) <= iota((LANES, LANES), 1)).astype(bf16)
    at, to = iota((wide, wide), 0), iota((wide, wide), 1)
    earlier = ((at // blocks == to // blocks) & (to < at)).astype(bf16)
    offset = owner_ref[...] ^ (code_ref[0] >> 1)
    group = jnp.where(offset < 2, offset, offset ^ (code_ref[0] & 1))
    hits = [(group == g).astype(f32) for g in range(groups)]
    stacked = jnp.concatenate(hits, axis=0).astype(bf16)
    inside = jnp.dot(stacked, upper, preferred_element_type=f32)
    totals = jnp.dot(stacked, jnp.ones((LANES, LANES), bf16), preferred_element_type=f32)
    carry = jnp.dot(earlier, totals.astype(bf16), preferred_element_type=f32)
    rank = inside + carry - 1.0
    slot = jnp.zeros((blocks, LANES), f32)
    for g in range(groups):
        slot = slot + hits[g] * (rank[g * blocks:(g + 1) * blocks] + float(g * capacity))
    slot_ref[...] = slot


def first_kernel(groups, capacity, wanted, slot_ref, row_ref, w_ref, bags_ref, out_ref, ext_ref):
    blocks = slot_ref.shape[0]
    lane = iota((LANES, LANES), 1)
    repeat = ((iota((LANES, LANES // 2), 0) >> 1) == iota((LANES, LANES // 2), 1)).astype(bf16)
    columns = jnp.concatenate(
        [(row_ref[...] >> 8).astype(f32), (row_ref[...] & 255).astype(f32), w_ref[...],
         jnp.zeros((LANES - 3 * blocks, LANES), f32)], axis=0).T
    for r in range(blocks):
        bag = jnp.dot(repeat, bags_ref[r * LANES // 2:(r + 1) * LANES // 2, :], preferred_element_type=f32)
        here = slice(r * LANES, (r + 1) * LANES)
        ext_ref[here, 0:LANES] = (bag * columns[:, 2 * blocks + r:2 * blocks + r + 1]).astype(bf16)
        high, low = columns[:, r:r + 1], columns[:, blocks + r:blocks + r + 1]
        ext_ref[here, LANES:2 * LANES] = jnp.where(
            lane == 0, high, jnp.where(lane == 1, low, 0.0)).astype(bf16)
    pack_groups(groups, capacity, wanted, slot_ref[...], ext_ref, out_ref)


def next_kernel(groups, capacity, wanted, slot_ref, ext_ref, *refs):
    out_ref = refs[-1]
    pack_groups(groups, capacity, wanted, slot_ref[...], ext_ref, out_ref)


def listed(wanted, capacity):
    return jax.ShapeDtypeStruct((len(wanted), capacity + PAD, LANES), bf16)


def find_slots(code, owner, groups, capacity):
    vmem = pl.BlockSpec(memory_space=pltpu.VMEM)
    return pl.pallas_call(
        functools.partial(rank_kernel, groups, capacity),
        out_shape=jax.ShapeDtypeStruct(owner.shape, f32),
        in_specs=[pl.BlockSpec(memory_space=pltpu.SMEM), vmem],
        out_specs=vmem,
        compiler_params=pltpu.CompilerParams(vmem_limit_bytes=VMEM_LIMIT),
        cost_estimate=pl.CostEstimate(flops=20_000_000_000, bytes_accessed=1024, transcendentals=0),
        name="find_slots",
    )(code, owner)


def pack_first(slot, local_row, lookup_weight, bags, groups, capacity, wanted):
    vmem = pl.BlockSpec(memory_space=pltpu.VMEM)
    return pl.pallas_call(
        functools.partial(first_kernel, groups, capacity, wanted),
        out_shape=[listed(wanted, capacity), jax.ShapeDtypeStruct((slot.size, 2 * LANES), bf16)],
        in_specs=[vmem] * 4,
        out_specs=[vmem, vmem],
        compiler_params=pltpu.CompilerParams(vmem_limit_bytes=VMEM_LIMIT),
        name="pack_first",
    )(slot, local_row, lookup_weight, bags)


def pack_next(slot, ext, groups, capacity, wanted, after=()):
    vmem = pl.BlockSpec(memory_space=pltpu.VMEM)
    return pl.pallas_call(
        functools.partial(next_kernel, groups, capacity, wanted),
        out_shape=listed(wanted, capacity),
        in_specs=[vmem, vmem] + [pl.BlockSpec(memory_space=pl.ANY)] * len(after),
        out_specs=vmem,
        compiler_params=pltpu.CompilerParams(vmem_limit_bytes=VMEM_LIMIT),
        cost_estimate=SMALL,
        name="pack_next",
    )(slot, ext, *after)


def add_kernel(capacity, lists, first, last, total, start, built, *refs):
    in_refs, refs = refs[:lists], list(refs[lists:])
    out_ref, rhs_ref = (refs[-1], refs[-2]) if built else refs[-2:]
    before = None if first else refs.pop(0)
    beside = refs.pop(0) if last else None
    half = total
    chunks = capacity // LANES
    highs, lows = [], []
    at = 0
    for ref in in_refs:
        for part in range(ref.shape[0] // (capacity + PAD)):
            base = part * (capacity + PAD)
            digits = ref[base + capacity:base + capacity + PAD, :].astype(f32)
            high = digits[0:chunks]
            upper = (high >= float(half // 256)).astype(f32)
            high = high - upper * float(half // 256)
            highs += [high[k:k + 1] for k in range(chunks)]
            lows += [digits[chunks + k:chunks + k + 1] for k in range(chunks)]
            if built:
                continue
            turned = jnp.concatenate([upper, jnp.zeros((LANES - chunks, LANES), f32)], axis=0).T
            for k in range(chunks):
                rows = ref[base + k * LANES:base + (k + 1) * LANES, :].astype(f32)
                above = turned[:, k:k + 1] > 0.5
                here = slice(at, at + LANES)
                rhs_ref[here, 0:LANES] = jnp.where(above, 0.0, rows).astype(bf16)
                rhs_ref[here, LANES:2 * LANES] = jnp.where(above, rows, 0.0).astype(bf16)
                at += LANES
    place = iota((256, LANES), 0, f32)
    for n in range(out_ref.shape[0] // 256):
        h = start + n
        picks = jnp.concatenate(
            [(place == jnp.where(hi == float(h), lo, -1.0)).astype(bf16) for hi, lo in zip(highs, lows)], axis=1)
        part = jnp.dot(picks, rhs_ref[...], preferred_element_type=f32)
        here = slice(h * 256, (h + 1) * 256)
        if before is not None:
            part = part + before[here, :]
        if beside is not None:
            part = part + beside[here, :]
        out_ref[n * 256:(n + 1) * 256, :] = part.astype(out_ref.dtype)


def add_lists(lists, before, beside, half, capacity, piece=0, pieces=1, after=(), rhs=None):
    vmem = pl.BlockSpec(memory_space=pltpu.VMEM)
    n = len(lists)
    depth = sum(value.shape[0] for value in lists) // (capacity + PAD) * capacity
    more = [value for value in (before, beside) if value is not None]
    out = jax.ShapeDtypeStruct((half // pieces, 2 * LANES), f32 if beside is None else bf16)
    product = jax.ShapeDtypeStruct((depth, 2 * LANES), bf16)
    results = pl.pallas_call(
        functools.partial(add_kernel, capacity, n, before is None, beside is not None, half, piece * (half // pieces // 256),
                          rhs is not None),
        out_shape=[out] if rhs is not None else [out, product] if beside is not None else [out],
        in_specs=[vmem] * (n + len(more)) + [pl.BlockSpec(memory_space=pl.ANY)] * len(after) + [vmem] * (rhs is not None),
        out_specs=[vmem, vmem] if rhs is None and beside is not None else [vmem],
        scratch_shapes=[pltpu.VMEM(product.shape, bf16)] if beside is None else [],
        input_output_aliases={n: 0} if beside is None and before is not None else {},
        compiler_params=pltpu.CompilerParams(vmem_limit_bytes=VMEM_LIMIT),
        cost_estimate=MEDIUM,
        name="add_lists",
    )(*lists, *more, *after, *([] if rhs is None else [rhs]))
    return results if beside is not None and rhs is None else results[0]


def update_kernel(first, own_ref, other_ref, weight_ref, accum_ref, *refs):
    new_weight_hbm, new_accum_hbm, out_ref, new_accum_ref, sems = refs[-5:]
    blocks = accum_ref.shape[0]
    span = own_ref.shape[0] // LANES
    lane = iota((LANES, LANES), 1)
    old = jnp.concatenate([accum_ref[...], jnp.zeros((LANES - blocks, LANES), f32)], axis=0).T
    new = old
    copies = []
    group = 4
    for side in range(2):
        base = side * (blocks // 2) + first * span

        def grad(n):
            at, to = slice(n * LANES, (n + 1) * LANES), slice(side * LANES, (side + 1) * LANES)
            return own_ref[at, to].astype(f32) + other_ref[at, to].astype(f32)

        for n in range(span):
            g = grad(n)
            new = jnp.where(lane == base + n, new + jnp.sum(g * g, axis=1, keepdims=True) * (1.0 / LANES), new)
        scale = step_size / (jnp.sqrt(new) + epsilon)
        for n in range(span):
            b = base + n
            out_ref[(side * span + n) * LANES:(side * span + n + 1) * LANES, :] = (
                weight_ref[b * LANES:(b + 1) * LANES, :] - grad(n) * scale[:, b:b + 1])
            if (n + 1) % group == 0:
                m = n + 1 - group
                copies.append(pltpu.make_async_copy(
                    out_ref.at[(side * span + m) * LANES:(side * span + n + 1) * LANES],
                    new_weight_hbm.at[(base + m) * LANES:(b + 1) * LANES], sems.at[len(copies)]))
                copies[-1].start()
    new_accum_ref[...] = new.T[:blocks]
    copies.append(pltpu.make_async_copy(new_accum_ref, new_accum_hbm, sems.at[len(copies)]))
    copies[-1].start()
    for copy in copies:
        copy.wait()


def update(piece, own, other, weight, accum, so_far):
    vmem, hbm = pl.BlockSpec(memory_space=pltpu.VMEM), pl.BlockSpec(memory_space=pltpu.HBM)
    more = [] if so_far is None else [so_far]
    return pl.pallas_call(
        functools.partial(update_kernel, piece),
        out_shape=[jax.ShapeDtypeStruct(weight.shape, f32), jax.ShapeDtypeStruct(accum.shape, f32)],
        in_specs=[vmem] * 4 + [hbm] * len(more),
        out_specs=[hbm, pl.BlockSpec(memory_space=pl.ANY)],
        scratch_shapes=[pltpu.VMEM((2 * own.shape[0], LANES), f32), pltpu.VMEM(accum.shape, f32),
                        pltpu.SemaphoreType.DMA((5,))],
        input_output_aliases={4: 0} if more else {},
        compiler_params=pltpu.CompilerParams(vmem_limit_bytes=VMEM_LIMIT),
        name="update",
    )(own, other, weight, accum, *more)


def tied(value, after):
    return value + (after[-1:, 0:LANES] * 0.0).astype(value.dtype)


def paired_body(shards, reps, grad_pooled, lookup_weight, owner, local_row, weight, accum):
    width = grad_pooled.shape[-1]
    lookups = lookup_weight.shape[0]
    capacity = (3 * lookups + 2 * shards - 1) // (2 * shards)
    half = weight.shape[0] // 2
    axes = ("shard", "rep")

    def permute(value, target):
        pairs = [(s * reps + r, target(s, r)) for s in range(shards) for r in range(reps)]
        return lax.ppermute(value, axes, pairs)

    to_core = functools.partial(permute, target=lambda s, r: s * reps + (r ^ 1))
    to_copy = functools.partial(permute, target=lambda s, r: s * reps + (r ^ 2))
    code = lax.axis_index("shard").astype(i32) * 2 + (lax.axis_index("rep").astype(i32) & 1)
    dense = (lookups // LANES, LANES)
    slot = find_slots(code.reshape(1), owner.reshape(dense), shards, capacity)

    def swapped(qs, pack_given, after):
        got = to_core(pack_given)
        keep = pack_next(slot, ext, shards, capacity, [2 * q for q in qs], after)
        return [jnp.concatenate([keep[n], got[n]], axis=0) for n in range(len(qs))]

    def send(q, payload):
        return permute(payload, lambda s, r: (s ^ (2 * q + (r & 1))) * reps + r)

    far = shards // 2 - 1
    near = [1, far - 1]
    given, ext = pack_first(slot, local_row.reshape(dense), lookup_weight.reshape(dense),
                            grad_pooled.reshape(-1, width), shards, capacity, [2 * far + 1])
    first = swapped([far], given, ())
    lists = {far: send(far, first[0])}
    given = pack_next(slot, ext, shards, capacity, [2 * q + 1 for q in near], first)
    got = to_core(given)
    kept = pack_next(slot, ext, shards, capacity, [2 * q for q in near], first)
    beside = pack_next(slot, ext, shards, capacity, [0, 1], [got])
    lists[0] = jnp.concatenate([beside[0], permute(beside[1], lambda s, r: (s ^ 1) * reps + r)], axis=0)
    for n, q in enumerate(near):
        lists[q] = send(q, jnp.concatenate([kept[n], got[n]], axis=0))

    last = far - 1
    there = to_copy(lists[0])
    own = add_lists([lists[0]], None, None, half, capacity)
    here_far = tied(lists[far], own)
    there_far = to_copy(here_far)
    here_near = tied(lists[1], here_far)
    there_near = to_copy(here_near)
    own = add_lists([here_far], own, None, half, capacity, after=[here_near])
    copy = add_lists([there], None, None, half, capacity, after=[here_near])
    here_last = tied(lists[last], own)
    there_last = to_copy(here_last)
    own = add_lists([here_near], own, None, half, capacity, after=[here_last])
    copy = add_lists([there_far], copy, None, half, capacity, after=[here_last])
    own = add_lists([here_last], own, None, half, capacity)
    copy = add_lists([there_near], copy, None, half, capacity)
    there = there_last

    pieces = 2
    total, rhs = add_lists([there], copy, own, half, capacity, 0, pieces)
    sums = [total] + [add_lists([there], copy, own, half, capacity, n, pieces, rhs=rhs) for n in range(1, pieces)]
    others = [to_core(value) for value in sums]
    new_weight, new_accum = None, accum.reshape(-1, LANES)
    for n in range(pieces):
        new_weight, new_accum = update(n, sums[n], others[n], weight, new_accum, new_weight)
    return new_weight, new_accum.reshape(-1)


def solution(mesh):
    shards, reps = mesh.shape["shard"], mesh.shape["rep"]
    in_specs = (
        P(("shard", "rep"), None, None),
        P(("shard", "rep")),
        P(("shard", "rep"), None),
        P(("shard", "rep")),
        P("shard", None),
        P("shard"),
    )
    out_specs = (P("shard", None), P("shard"))
    paired = reps == 4 and shards == 8
    body = functools.partial(paired_body, shards, reps) if paired else general_body
    return jax.shard_map(body, mesh=mesh, in_specs=in_specs, out_specs=out_specs, check_vma=False)
```

```python
import functools

import jax
import jax.numpy as jnp
from jax import lax
from jax.experimental import pallas as pl
from jax.experimental.pallas import tpu as pltpu
from jax.sharding import PartitionSpec as P

step_size = 0.25
epsilon = 1e-08
f32, bf16, i32 = jnp.float32, jnp.bfloat16, jnp.int32
LANES = 128
PAD = 16
VMEM_LIMIT = 48 * 1024 * 1024
MEDIUM = pl.CostEstimate(flops=100_000_000, bytes_accessed=1024, transcendentals=0)
SMALL = pl.CostEstimate(flops=1024, bytes_accessed=1024, transcendentals=0)


def adagrad(weight, accum, table_grad):
    new_accum = accum + jnp.mean(table_grad * table_grad, axis=1)
    new_weight = weight - step_size * table_grad / (jnp.sqrt(new_accum)[:, None] + epsilon)
    return (new_weight, new_accum)


def general_body(grad_pooled, lookup_weight, owner, local_row, weight, accum):
    width = grad_pooled.shape[-1]
    lookups = lookup_weight.shape[0]
    pooling = lookups // (grad_pooled.shape[0] * grad_pooled.shape[1])
    shards = lax.axis_size("shard")
    capacity = (3 * lookups + 2 * shards - 1) // (2 * shards)
    bags = grad_pooled.reshape(-1, width).astype(f32)
    rows = (bags[:, None, :] * lookup_weight.reshape(-1, pooling, 1)).reshape(lookups, width)
    rows = rows.astype(bf16)
    target_shard = owner[:, 0]
    hits = (target_shard[:, None] == jnp.arange(shards, dtype=i32)[None, :]).astype(i32)
    ranks = jnp.sum(jnp.cumsum(hits, axis=0) * hits, axis=1) - 1
    slots = target_shard * capacity + ranks
    outgoing = jnp.zeros((shards * capacity, width), bf16).at[slots].set(rows)
    row_ids = jnp.full((shards * capacity,), -1, i32).at[slots].set(local_row)
    received, received_ids = (
        lax.all_to_all(outgoing.reshape(shards, capacity, width), "shard", split_axis=0, concat_axis=0, tiled=True),
        lax.all_to_all(row_ids.reshape(shards, capacity), "shard", split_axis=0, concat_axis=0, tiled=True),
    )
    flat_rows = received.reshape(-1, width)
    flat_ids = received_ids.reshape(-1)
    window_rows = weight.shape[0]
    span = 512
    starts = jnp.arange(window_rows // span, dtype=i32) * span

    def one_block(start):
        shifted = flat_ids - start
        onehot = (jnp.arange(span, dtype=i32)[:, None] == shifted[None, :]).astype(bf16)
        return jnp.dot(onehot, flat_rows, preferred_element_type=f32)

    partial_grad = lax.map(one_block, starts).reshape(window_rows, width)
    table_grad = lax.psum(partial_grad, "rep")
    return adagrad(weight, accum, table_grad)


def iota(shape, dim, dtype=i32):
    return lax.broadcasted_iota(i32, shape, dim).astype(dtype)


def pack_groups(groups, capacity, wanted, slot, ext_ref, out_ref):
    blocks = slot.shape[0]
    chunks = capacity // LANES
    place = iota((LANES, LANES), 0, f32)
    for n, g in enumerate(wanted):
        high, low = [], []
        for k in range(chunks):
            moved = slot - float(g * capacity + k * LANES)
            picks = jnp.concatenate(
                [(place == moved[r:r + 1, :]).astype(bf16) for r in range(blocks)], axis=1)
            packed = jnp.dot(picks, ext_ref[...], preferred_element_type=f32)
            out_ref[n, k * LANES:(k + 1) * LANES, :] = packed[:, :LANES].astype(bf16)
            turned = packed[:, LANES:].T
            high.append(turned[0:1])
            low.append(turned[1:2])
        out_ref[n, capacity:capacity + PAD, :] = jnp.concatenate(
            high + low + [jnp.zeros((PAD - 2 * chunks, LANES), f32)], axis=0).astype(bf16)


def rank_kernel(groups, capacity, code_ref, owner_ref, slot_ref):
    blocks = slot_ref.shape[0]
    wide = groups * blocks
    upper = (iota((LANES, LANES), 0) <= iota((LANES, LANES), 1)).astype(bf16)
    at, to = iota((wide, wide), 0), iota((wide, wide), 1)
    earlier = ((at // blocks == to // blocks) & (to < at)).astype(bf16)
    offset = owner_ref[...] ^ (code_ref[0] >> 1)
    group = jnp.where(offset < 2, offset, offset ^ (code_ref[0] & 1))
    hits = [(group == g).astype(f32) for g in range(groups)]
    stacked = jnp.concatenate(hits, axis=0).astype(bf16)
    inside = jnp.dot(stacked, upper, preferred_element_type=f32)
    totals = jnp.dot(stacked, jnp.ones((LANES, LANES), bf16), preferred_element_type=f32)
    carry = jnp.dot(earlier, totals.astype(bf16), preferred_element_type=f32)
    rank = inside + carry - 1.0
    slot = jnp.zeros((blocks, LANES), f32)
    for g in range(groups):
        slot = slot + hits[g] * (rank[g * blocks:(g + 1) * blocks] + float(g * capacity))
    slot_ref[...] = slot


def first_kernel(groups, capacity, wanted, slot_ref, row_ref, w_ref, bags_ref, out_ref, ext_ref):
    blocks = slot_ref.shape[0]
    lane = iota((LANES, LANES), 1)
    repeat = ((iota((LANES, LANES // 2), 0) >> 1) == iota((LANES, LANES // 2), 1)).astype(bf16)
    columns = jnp.concatenate(
        [(row_ref[...] >> 8).astype(f32), (row_ref[...] & 255).astype(f32), w_ref[...],
         jnp.zeros((LANES - 3 * blocks, LANES), f32)], axis=0).T
    for r in range(blocks):
        bag = jnp.dot(repeat, bags_ref[r * LANES // 2:(r + 1) * LANES // 2, :], preferred_element_type=f32)
        here = slice(r * LANES, (r + 1) * LANES)
        ext_ref[here, 0:LANES] = (bag * columns[:, 2 * blocks + r:2 * blocks + r + 1]).astype(bf16)
        high, low = columns[:, r:r + 1], columns[:, blocks + r:blocks + r + 1]
        ext_ref[here, LANES:2 * LANES] = jnp.where(
            lane == 0, high, jnp.where(lane == 1, low, 0.0)).astype(bf16)
    pack_groups(groups, capacity, wanted, slot_ref[...], ext_ref, out_ref)


def next_kernel(groups, capacity, wanted, slot_ref, ext_ref, *refs):
    out_ref = refs[-1]
    pack_groups(groups, capacity, wanted, slot_ref[...], ext_ref, out_ref)


def listed(wanted, capacity):
    return jax.ShapeDtypeStruct((len(wanted), capacity + PAD, LANES), bf16)


def find_slots(code, owner, groups, capacity):
    vmem = pl.BlockSpec(memory_space=pltpu.VMEM)
    return pl.pallas_call(
        functools.partial(rank_kernel, groups, capacity),
        out_shape=jax.ShapeDtypeStruct(owner.shape, f32),
        in_specs=[pl.BlockSpec(memory_space=pltpu.SMEM), vmem],
        out_specs=vmem,
        compiler_params=pltpu.CompilerParams(vmem_limit_bytes=VMEM_LIMIT),
        cost_estimate=pl.CostEstimate(flops=20_000_000_000, bytes_accessed=1024, transcendentals=0),
        name="find_slots",
    )(code, owner)


def pack_first(slot, local_row, lookup_weight, bags, groups, capacity, wanted):
    vmem = pl.BlockSpec(memory_space=pltpu.VMEM)
    return pl.pallas_call(
        functools.partial(first_kernel, groups, capacity, wanted),
        out_shape=[listed(wanted, capacity), jax.ShapeDtypeStruct((slot.size, 2 * LANES), bf16)],
        in_specs=[vmem] * 4,
        out_specs=[vmem, vmem],
        compiler_params=pltpu.CompilerParams(vmem_limit_bytes=VMEM_LIMIT),
        name="pack_first",
    )(slot, local_row, lookup_weight, bags)


def pack_next(slot, ext, groups, capacity, wanted, after=()):
    vmem = pl.BlockSpec(memory_space=pltpu.VMEM)
    return pl.pallas_call(
        functools.partial(next_kernel, groups, capacity, wanted),
        out_shape=listed(wanted, capacity),
        in_specs=[vmem, vmem] + [pl.BlockSpec(memory_space=pl.ANY)] * len(after),
        out_specs=vmem,
        compiler_params=pltpu.CompilerParams(vmem_limit_bytes=VMEM_LIMIT),
        cost_estimate=SMALL,
        name="pack_next",
    )(slot, ext, *after)


def add_kernel(capacity, lists, first, last, total, start, built, *refs):
    in_refs, refs = refs[:lists], list(refs[lists:])
    out_ref, rhs_ref = (refs[-1], refs[-2]) if built else refs[-2:]
    before = None if first else refs.pop(0)
    beside = refs.pop(0) if last else None
    half = total
    chunks = capacity // LANES
    highs, lows = [], []
    at = 0
    for ref in in_refs:
        for part in range(ref.shape[0] // (capacity + PAD)):
            base = part * (capacity + PAD)
            digits = ref[base + capacity:base + capacity + PAD, :].astype(f32)
            high = digits[0:chunks]
            upper = (high >= float(half // 256)).astype(f32)
            high = high - upper * float(half // 256)
            highs += [high[k:k + 1] for k in range(chunks)]
            lows += [digits[chunks + k:chunks + k + 1] for k in range(chunks)]
            if built:
                continue
            turned = jnp.concatenate([upper, jnp.zeros((LANES - chunks, LANES), f32)], axis=0).T
            for k in range(chunks):
                rows = ref[base + k * LANES:base + (k + 1) * LANES, :]
                above = rows * jnp.broadcast_to(turned[:, k:k + 1], (LANES, LANES)).astype(bf16)
                here = slice(at, at + LANES)
                rhs_ref[here, 0:LANES] = rows - above
                rhs_ref[here, LANES:2 * LANES] = above
                at += LANES
    place = iota((256, LANES), 0, f32)
    for n in range(out_ref.shape[0] // 256):
        h = start + n
        picks = jnp.concatenate(
            [(place == jnp.where(hi == float(h), lo, -1.0)).astype(bf16) for hi, lo in zip(highs, lows)], axis=1)
        part = jnp.dot(picks, rhs_ref[...], preferred_element_type=f32)
        here = slice(h * 256, (h + 1) * 256)
        if before is not None:
            part = part + before[here, :]
        if beside is not None:
            part = part + beside[here, :]
        out_ref[n * 256:(n + 1) * 256, :] = part.astype(out_ref.dtype)


def add_lists(lists, before, beside, half, capacity, piece=0, pieces=1, after=(), rhs=None):
    vmem = pl.BlockSpec(memory_space=pltpu.VMEM)
    n = len(lists)
    depth = sum(value.shape[0] for value in lists) // (capacity + PAD) * capacity
    more = [value for value in (before, beside) if value is not None]
    out = jax.ShapeDtypeStruct((half // pieces, 2 * LANES), f32 if beside is None else bf16)
    product = jax.ShapeDtypeStruct((depth, 2 * LANES), bf16)
    results = pl.pallas_call(
        functools.partial(add_kernel, capacity, n, before is None, beside is not None, half, piece * (half // pieces // 256),
                          rhs is not None),
        out_shape=[out] if rhs is not None else [out, product] if beside is not None else [out],
        in_specs=[vmem] * (n + len(more)) + [pl.BlockSpec(memory_space=pl.ANY)] * len(after) + [vmem] * (rhs is not None),
        out_specs=[vmem, vmem] if rhs is None and beside is not None else [vmem],
        scratch_shapes=[pltpu.VMEM(product.shape, bf16)] if beside is None else [],
        input_output_aliases={n: 0} if beside is None and before is not None else {},
        compiler_params=pltpu.CompilerParams(vmem_limit_bytes=VMEM_LIMIT),
        cost_estimate=MEDIUM,
        name="add_lists",
    )(*lists, *more, *after, *([] if rhs is None else [rhs]))
    return results if beside is not None and rhs is None else results[0]


def update_kernel(first, own_ref, other_ref, weight_ref, accum_ref, *refs):
    new_weight_hbm, new_accum_hbm, out_ref, new_accum_ref, sems = refs[-5:]
    blocks = accum_ref.shape[0]
    span = own_ref.shape[0] // LANES
    lane = iota((LANES, LANES), 1)
    old = jnp.concatenate([accum_ref[...], jnp.zeros((LANES - blocks, LANES), f32)], axis=0).T
    new = old
    copies = []
    group = 4
    for side in range(2):
        base = side * (blocks // 2) + first * span

        def grad(n):
            at, to = slice(n * LANES, (n + 1) * LANES), slice(side * LANES, (side + 1) * LANES)
            return own_ref[at, to].astype(f32) + other_ref[at, to].astype(f32)

        for n in range(span):
            g = grad(n)
            new = jnp.where(lane == base + n, new + jnp.sum(g * g, axis=1, keepdims=True) * (1.0 / LANES), new)
        scale = step_size / (jnp.sqrt(new) + epsilon)
        for n in range(span):
            b = base + n
            out_ref[(side * span + n) * LANES:(side * span + n + 1) * LANES, :] = (
                weight_ref[b * LANES:(b + 1) * LANES, :] - grad(n) * scale[:, b:b + 1])
            if (n + 1) % group == 0:
                m = n + 1 - group
                copies.append(pltpu.make_async_copy(
                    out_ref.at[(side * span + m) * LANES:(side * span + n + 1) * LANES],
                    new_weight_hbm.at[(base + m) * LANES:(b + 1) * LANES], sems.at[len(copies)]))
                copies[-1].start()
    new_accum_ref[...] = new.T[:blocks]
    copies.append(pltpu.make_async_copy(new_accum_ref, new_accum_hbm, sems.at[len(copies)]))
    copies[-1].start()
    for copy in copies:
        copy.wait()


def update(piece, own, other, weight, accum, so_far):
    vmem, hbm = pl.BlockSpec(memory_space=pltpu.VMEM), pl.BlockSpec(memory_space=pltpu.HBM)
    more = [] if so_far is None else [so_far]
    return pl.pallas_call(
        functools.partial(update_kernel, piece),
        out_shape=[jax.ShapeDtypeStruct(weight.shape, f32), jax.ShapeDtypeStruct(accum.shape, f32)],
        in_specs=[vmem] * 4 + [hbm] * len(more),
        out_specs=[hbm, pl.BlockSpec(memory_space=pl.ANY)],
        scratch_shapes=[pltpu.VMEM((2 * own.shape[0], LANES), f32), pltpu.VMEM(accum.shape, f32),
                        pltpu.SemaphoreType.DMA((5,))],
        input_output_aliases={4: 0} if more else {},
        compiler_params=pltpu.CompilerParams(vmem_limit_bytes=VMEM_LIMIT),
        name="update",
    )(own, other, weight, accum, *more)


def tied(value, after):
    return value + (after[-1:, 0:LANES] * 0.0).astype(value.dtype)


def paired_body(shards, reps, grad_pooled, lookup_weight, owner, local_row, weight, accum):
    width = grad_pooled.shape[-1]
    lookups = lookup_weight.shape[0]
    capacity = (3 * lookups + 2 * shards - 1) // (2 * shards)
    half = weight.shape[0] // 2
    axes = ("shard", "rep")

    def permute(value, target):
        pairs = [(s * reps + r, target(s, r)) for s in range(shards) for r in range(reps)]
        return lax.ppermute(value, axes, pairs)

    to_core = functools.partial(permute, target=lambda s, r: s * reps + (r ^ 1))
    to_copy = functools.partial(permute, target=lambda s, r: s * reps + (r ^ 2))
    code = lax.axis_index("shard").astype(i32) * 2 + (lax.axis_index("rep").astype(i32) & 1)
    dense = (lookups // LANES, LANES)
    slot = find_slots(code.reshape(1), owner.reshape(dense), shards, capacity)

    def swapped(qs, pack_given, after):
        got = to_core(pack_given)
        keep = pack_next(slot, ext, shards, capacity, [2 * q for q in qs], after)
        return [jnp.concatenate([keep[n], got[n]], axis=0) for n in range(len(qs))]

    def send(q, payload):
        return permute(payload, lambda s, r: (s ^ (2 * q + (r & 1))) * reps + r)

    far = shards // 2 - 1
    near = [1, far - 1]
    given, ext = pack_first(slot, local_row.reshape(dense), lookup_weight.reshape(dense),
                            grad_pooled.reshape(-1, width), shards, capacity, [2 * far + 1])
    first = swapped([far], given, ())
    lists = {far: send(far, first[0])}
    given = pack_next(slot, ext, shards, capacity, [2 * q + 1 for q in near], first)
    got = to_core(given)
    kept = pack_next(slot, ext, shards, capacity, [2 * q for q in near], first)
    beside = pack_next(slot, ext, shards, capacity, [0, 1], [got])
    lists[0] = jnp.concatenate([beside[0], permute(beside[1], lambda s, r: (s ^ 1) * reps + r)], axis=0)
    for n, q in enumerate(near):
        lists[q] = send(q, jnp.concatenate([kept[n], got[n]], axis=0))

    last = far - 1
    there = to_copy(lists[0])
    own = add_lists([lists[0]], None, None, half, capacity)
    here_far = tied(lists[far], own)
    there_far = to_copy(here_far)
    here_near = tied(lists[1], here_far)
    there_near = to_copy(here_near)
    own = add_lists([here_far], own, None, half, capacity, after=[here_near])
    copy = add_lists([there], None, None, half, capacity, after=[here_near])
    here_last = tied(lists[last], own)
    there_last = to_copy(here_last)
    own = add_lists([here_near], own, None, half, capacity, after=[here_last])
    copy = add_lists([there_far], copy, None, half, capacity, after=[here_last])
    own = add_lists([here_last], own, None, half, capacity)
    copy = add_lists([there_near], copy, None, half, capacity)
    there = there_last

    pieces = 2
    total, rhs = add_lists([there], copy, own, half, capacity, 0, pieces)
    sums = [total] + [add_lists([there], copy, own, half, capacity, n, pieces, rhs=rhs) for n in range(1, pieces)]
    others = [to_core(value) for value in sums]
    new_weight, new_accum = None, accum.reshape(-1, LANES)
    for n in range(pieces):
        new_weight, new_accum = update(n, sums[n], others[n], weight, new_accum, new_weight)
    return new_weight, new_accum.reshape(-1)


def solution(mesh):
    shards, reps = mesh.shape["shard"], mesh.shape["rep"]
    in_specs = (
        P(("shard", "rep"), None, None),
        P(("shard", "rep")),
        P(("shard", "rep"), None),
        P(("shard", "rep")),
        P("shard", None),
        P("shard"),
    )
    out_specs = (P("shard", None), P("shard"))
    paired = reps == 4 and shards == 8
    body = functools.partial(paired_body, shards, reps) if paired else general_body
    return jax.shard_map(body, mesh=mesh, in_specs=in_specs, out_specs=out_specs, check_vma=False)
```
